32 devices in a mesh: rep: 8 (over z, x), grp: 4 (over y, core).
Axes of the slice: x: 2, y: 2, z: 4, core: 2. Of those that a mesh axis runs over, the one named last changes fastest.
Arguments:
- tokens: bfloat16 [8, 2048, 768], P('rep', 'grp'), may hold values from -6 to 6
- segment_ids: int32 [8, 2048], P('rep'), may hold values from 0 to 9, as said below
- w_qkv: bfloat16 [768, 2304], P('grp'), may hold values from -0.21875 to 0.21875
- w_out: bfloat16 [768, 768], P('grp'), may hold values from -1.75 to 1.75
- w_up: bfloat16 [768, 3072], P('grp'), may hold values from -0.21875 to 0.21875
- w_down: bfloat16 [3072, 768], P('grp'), may hold values from -0.109375 to 0.109375
- norm_gains: float32 [2, 768], replicated, may hold values from 0.5 to 1.5
- norm_shifts: float32 [2, 768], replicated, may hold values from -1.2 to 1.2
- proj_biases: float32 [4, 768], replicated, may hold values from -1.2 to 1.2
- up_bias: float32 [3072], replicated, may hold values from -1.8 to 1.8
- cotangent: bfloat16 [8, 2048, 768], P('rep', 'grp'), may hold values from -6 to 6
Outputs:
- block_out: bfloat16 [8, 2048, 768], P('rep', 'grp')
- input_grad: float32 [8, 2048, 768], P('rep', 'grp')
- grad_qkv: float32 [768, 2304], P('grp')
- grad_out: float32 [768, 768], P('grp')
- grad_up: float32 [768, 3072], P('grp')
- grad_down: float32 [3072, 768], P('grp')
- grad_gains: float32 [2, 768], replicated
- grad_shifts: float32 [2, 768], replicated
- grad_biases: float32 [4, 768], replicated
- grad_up_bias: float32 [3072], replicated
The draws below stay inside these ranges and needn't reach their ends.
Inputs may be any that keep to these rules, and one draw needn't show every extreme that they name: `segment_ids`: in each sequence the ids start at 0 and never fall. In one sequence, drawn from the seed, there are three documents and the middle one begins within the first 512 tokens and ends within the last 512; in the others there are ten documents, each but the last of 102 to 204 tokens.
All inputs are finite; a program needn't handle non-finite values.
Results may differ from the reference program's by a relative error of at most 0.017.
Values may be sent and summed in bfloat16 or wider, within the bound.
No kernel may reach another device: no remote copies, remote signals or barrier semaphores. Data moves between devices by JAX's collectives and lax.ppermute only.
A program may use at most 128 MiB of HBM per device.

```python
import math
import jax
import jax.numpy as jnp
from jax import lax

D = 768
H = 12
HD = 64
FF = 3072
SEQ = 2048
SEQS = 8
TOK_DEV = 512


def draw_segment_ids(key, part):
    key = jax.random.fold_in(key, 11)
    key_len, key_one, key_two, key_pick = jax.random.split(key, 4)
    positions = jnp.arange(SEQ, dtype=jnp.int32)
    doc_lengths = jax.random.randint(key_len, (SEQS, 9), SEQ // 20, SEQ // 10 + 1).astype(jnp.int32)
    doc_cuts = jnp.cumsum(doc_lengths, axis=1).astype(jnp.int32)
    random_ids = jnp.sum((positions[None, :, None] >= doc_cuts[:, None, :]).astype(jnp.int32), axis=2)
    cut_one = jax.random.randint(key_one, (), max(1, SEQ // 64), TOK_DEV).astype(jnp.int32)
    cut_two = jax.random.randint(key_two, (), SEQ - TOK_DEV + 1, SEQ - SEQ // 64 + 1).astype(jnp.int32)
    spanning_ids = (positions >= cut_one).astype(jnp.int32) + (positions >= cut_two).astype(jnp.int32)
    chosen = jax.random.randint(key_pick, (), 0, SEQS).astype(jnp.int32)
    row_index = jnp.arange(SEQS, dtype=jnp.int32)[:, None]
    total_ids = jnp.where(row_index == chosen, spanning_ids[None, :], random_ids)
    return total_ids.astype(jnp.int32)


def block_levels(key, dims, cuts, low, largest):
    loudness = 1.0
    for position, parts in cuts:
        draws = jax.random.uniform(jax.random.fold_in(jax.random.fold_in(key, 6), position), (parts,), jnp.float32, low / len(cuts), largest / len(cuts))
        loudness = loudness * jnp.repeat(jnp.exp(draws), dims[position] // parts).reshape((-1,) + (1,) * (len(dims) - 1 - position))
    return loudness


def noise(rng, dims, width, most, cuts=(), kind=jnp.bfloat16):
    loudness = block_levels(rng, dims, cuts, -0.22, 0.18) if cuts else 1.0
    values = jax.random.normal(rng, dims, jnp.float32) * width * loudness
    return jnp.minimum(jnp.maximum(values, -most), most).astype(kind)


def setup_inputs(seed: int = 0) -> dict:
    key_list = jax.random.split(jax.random.key(seed), 12)
    tokens = noise(key_list[0], (SEQS, SEQ, D), 1.0, 6.0, ((0, 8), (1, 4)))
    segment_ids = draw_segment_ids(jax.random.fold_in(key_list[11], 71), 0)
    w_qkv = noise(key_list[2], (D, 3 * D), D ** -0.5, 0.21875, ((0, 4),))
    w_out = noise(key_list[3], (D, D), (D // 64) ** -0.5, 1.75, ((0, 4),))
    w_up = noise(key_list[4], (D, FF), D ** -0.5, 0.21875, ((0, 4),))
    w_down = noise(key_list[5], (FF, D), FF ** -0.5, 0.109375, ((0, 4),))
    norm_gains = jnp.clip(1.0 + 0.1 * jax.random.normal(key_list[6], (2, D), jnp.float32), 0.5, 1.5)
    norm_shifts = noise(key_list[7], (2, D), 0.2, 1.2, (), jnp.float32)
    proj_biases = noise(key_list[8], (4, D), 0.2, 1.2, (), jnp.float32)
    up_bias = noise(key_list[9], (FF,), 0.3, 1.8, (), jnp.float32)
    cotangent = noise(key_list[10], (SEQS, SEQ, D), 1.0, 6.0, ((0, 8), (1, 4)))
    return dict(tokens=tokens, segment_ids=segment_ids, w_qkv=w_qkv, w_out=w_out, w_up=w_up, w_down=w_down, norm_gains=norm_gains, norm_shifts=norm_shifts, proj_biases=proj_biases, up_bias=up_bias, cotangent=cotangent)


@jax.custom_vjp
def low(v):
    return lax.optimization_barrier(v.astype(jnp.bfloat16)).astype(jnp.float32)

@jax.custom_vjp
def low_back(v):
    return v

def low_keep(v):
    return (low(v), None)

def low_pass(kept, grad):
    return (grad,)

def back_keep(v):
    return (v, None)

def back_low(kept, grad):
    return (low(grad),)
low.defvjp(low_keep, low_pass)
low_back.defvjp(back_keep, back_low)

def layer_norm(values, gain_row, shift_row):
    centre = values - lax.optimization_barrier(jnp.mean(values, axis=-1, keepdims=True))
    spread = lax.optimization_barrier(jnp.mean(centre * centre, axis=-1, keepdims=True))
    return centre * lax.rsqrt(spread + 1e-05) * gain_row + shift_row

def attention(queries, key_rows, value_rows, segments):
    block_len = min(512, SEQ)
    scale_factor = 1.0 / math.sqrt(HD)
    positions = jnp.arange(SEQ, dtype=jnp.int32)

    def one_block(first_row):
        query_block = lax.dynamic_slice_in_dim(queries, first_row, block_len, 0)
        query_pos = lax.dynamic_slice_in_dim(positions, first_row, block_len, 0)
        query_seg = lax.dynamic_slice_in_dim(segments, first_row, block_len, 0)
        scores = jnp.einsum('qhd,khd->hqk', query_block, key_rows, precision=lax.Precision.HIGHEST) * scale_factor
        allowed = (positions[None, :] <= query_pos[:, None]) & (segments[None, :] == query_seg[:, None])
        scores = low_back(jnp.where(allowed[None], scores, -1e+30))
        weights = low(jax.nn.softmax(scores, axis=-1))
        return jnp.einsum('hqk,khd->qhd', weights, value_rows, precision=lax.Precision.HIGHEST)
    starts = jnp.arange(SEQ // block_len, dtype=jnp.int32) * block_len
    blocks = lax.map(jax.checkpoint(one_block), starts)
    return blocks.reshape(SEQ, D)

def forward(tokens_row, segments, w_qkv, w_out, w_up, w_down, norm_gains, norm_shifts, proj_biases, up_bias):
    normed = low(layer_norm(tokens_row, norm_gains[0], norm_shifts[0]))
    projected = jnp.dot(normed, w_qkv, precision=lax.Precision.HIGHEST)
    queries = low(low_back(projected[:, :D] + proj_biases[0]))
    key_rows = low(low_back(projected[:, D:2 * D]))
    value_rows = low(low_back(projected[:, 2 * D:] + proj_biases[1]))
    attended = attention(queries.reshape(SEQ, H, HD), key_rows.reshape(SEQ, H, HD), value_rows.reshape(SEQ, H, HD), segments)
    attended = low(low_back(attended))
    branch = low_back(jnp.dot(attended, w_out, precision=lax.Precision.HIGHEST) + proj_biases[2])
    middle = tokens_row + branch
    second = low(layer_norm(middle, norm_gains[1], norm_shifts[1]))
    hidden_pre = low_back(jnp.dot(second, w_up, precision=lax.Precision.HIGHEST) + up_bias)
    hidden = low(jax.nn.gelu(hidden_pre))
    return middle + jnp.dot(hidden, w_down, precision=lax.Precision.HIGHEST) + proj_biases[3]

def reference(tokens, segment_ids, w_qkv, w_out, w_up, w_down, norm_gains, norm_shifts, proj_biases, up_bias, cotangent):
    params = (w_qkv.astype(jnp.float32), w_out.astype(jnp.float32), w_up.astype(jnp.float32), w_down.astype(jnp.float32), norm_gains.astype(jnp.float32), norm_shifts.astype(jnp.float32), proj_biases.astype(jnp.float32), up_bias.astype(jnp.float32))

    def one_sequence(totals, sequence):
        tokens_row, segments, cot_row = sequence

        def forward_row(row_values, *weights):
            return forward(row_values, segments, *weights)
        outputs, pullback = jax.vjp(forward_row, tokens_row.astype(jnp.float32), *params)
        gradients = pullback(cot_row.astype(jnp.float32))
        totals = tuple((summed + gradient for summed, gradient in zip(totals, gradients[1:])))
        return (totals, (outputs.astype(jnp.bfloat16), gradients[0]))
    start_sums = tuple((jnp.zeros(weight.shape, jnp.float32) for weight in params))
    totals, (outputs, input_grad) = lax.scan(one_sequence, start_sums, (tokens, segment_ids, cotangent))
    return (outputs, input_grad, totals[0], totals[1], totals[2], totals[3], totals[4], totals[5], totals[6], totals[7])
```

```python
import functools
import math

import jax
import jax.numpy as jnp
from jax import lax
from jax.experimental import pallas as pl
from jax.experimental.pallas import tpu as pltpu
from jax.sharding import PartitionSpec as P

D = 768
H = 12
HD = 64
PAIRS = H // 2
LANES = 2 * HD
NEG = -1e30
SCALE = 1.0 / math.sqrt(HD)
F32 = jnp.float32
BF16 = jnp.bfloat16


def layer_norm(values, gain_row, shift_row):
    centre = values - jnp.mean(values, axis=-1, keepdims=True)
    spread = jnp.mean(centre * centre, axis=-1, keepdims=True)
    return centre * lax.rsqrt(spread + 1e-05) * gain_row + shift_row


def add_rows(left, piece):
    return jnp.dot(left, piece, preferred_element_type=F32)


def back_rows(right, piece):
    return jnp.einsum("te,ce->tc", right, piece, preferred_element_type=F32)


def token_product(left, right):
    return jnp.einsum("tc,te->ce", left, right, preferred_element_type=F32)


def swap(value, axis, size, mask):
    return lax.ppermute(value, axis, [(i, i ^ mask) for i in range(size)])


def bits_of(size):
    return size.bit_length() - 1


def gather_near(value, size):
    blocks = value[None]
    for bit in list(range(1, bits_of(size))) + [0]:
        blocks = jnp.concatenate([blocks, swap(blocks, "grp", size, 1 << bit)], axis=0)
    return blocks


def gather_later(value, size):
    blocks = value[None]
    for bit in list(range(1, bits_of(size))) + [0]:
        mask = 1 << bit
        if bit == 0:
            pairs = [(i, i ^ 1) for i in range(size)]
        else:
            pairs = [(i, i ^ mask) for i in range(size) if i & mask]
        blocks = jnp.concatenate([blocks, lax.ppermute(blocks, "grp", pairs)], axis=0)
    return blocks


def block_place(block, me, size):
    near = block ^ me
    return (near >> 1) | ((near & 1) << (bits_of(size) - 1))


def gather_weight(weight, me, rep, size, reps):
    rows, columns = weight.shape
    half = rows // 2
    side = rep & 1
    blocks = weight[None]
    for bit in range(1, bits_of(size)):
        part = lax.dynamic_slice_in_dim(blocks, side * half, half, 1)
        got = swap(part, "grp", size, 1 << bit)
        more = swap(got, "rep", reps, 1)
        low, high = jnp.where(side == 0, got, more), jnp.where(side == 0, more, got)
        blocks = jnp.concatenate([blocks, jnp.concatenate([low, high], axis=1)], axis=0)
    other = swap(blocks, "grp", size, 1)
    whole = jnp.zeros((size, rows, columns), weight.dtype)
    for place in range(size // 2):
        near = place << 1
        whole = lax.dynamic_update_slice(whole, blocks[place][None], (me ^ near, 0, 0))
        whole = lax.dynamic_update_slice(whole, other[place][None], (me ^ (near | 1), 0, 0))
    return whole.reshape(size * rows, columns)


def total_grad(left, right, me, rep, size, reps):
    rows = left.shape[1] // size
    columns = right.shape[1]
    core = me & 1
    strips = [left[:, i * rows : (i + 1) * rows] for i in range(size)]
    even = jnp.concatenate(strips[0::2], axis=1)
    odd = jnp.concatenate(strips[1::2], axis=1)
    theirs = token_product(jnp.where(core == 0, odd, even), right).astype(BF16)
    got = swap(theirs, "grp", size, 1)
    part = token_product(jnp.where(core == 0, even, odd), right) + got.astype(F32)
    part = part.astype(BF16).reshape(size // 2, rows, columns)
    for bit in range(bits_of(size) - 1, 0, -1):
        split = part.reshape(2, part.shape[0] // 2, rows, columns)
        side = (me >> bit) & 1
        send = lax.dynamic_index_in_dim(split, 1 - side, 0, keepdims=False)
        keep = lax.dynamic_index_in_dim(split, side, 0, keepdims=False)
        part = (keep.astype(F32) + swap(send, "grp", size, 1 << bit).astype(F32)).astype(BF16)
    part = part[0]
    for bit in range(bits_of(reps)):
        side = (rep >> bit) & 1
        half = part.shape[0] // 2
        send = lax.dynamic_slice_in_dim(part, (1 - side) * half, half, 0)
        keep = lax.dynamic_slice_in_dim(part, side * half, half, 0)
        part = (keep.astype(F32) + swap(send, "rep", reps, 1 << bit).astype(F32)).astype(BF16)
    for bit in range(bits_of(reps) - 1, -1, -1):
        side = (rep >> bit) & 1
        got = swap(part, "rep", reps, 1 << bit)
        low, high = jnp.where(side == 0, part, got), jnp.where(side == 0, got, part)
        part = jnp.concatenate([low, high], axis=0)
    return part.astype(F32)


def total_vector(value, size, reps):
    value = value + swap(value, "grp", size, 1)
    for bit in range(1, bits_of(size)):
        value = value + swap(value, "grp", size, 1 << bit)
    for bit in range(bits_of(reps)):
        value = value + swap(value, "rep", reps, 1 << bit)
    return value


def dot_nt(left, right):
    return lax.dot_general(left, right, (((1,), (1,)), ((), ())), preferred_element_type=F32)


def dot_nn(left, right):
    return lax.dot_general(left, right, (((1,), (0,)), ((), ())), preferred_element_type=F32)


def one_head(pair, head):
    lane = lax.broadcasted_iota(jnp.int32, pair.shape, 1)
    inside = (lane < HD) if head == 0 else (lane >= HD)
    return jnp.where(inside, pair, jnp.zeros_like(pair))


def per_head(first, second, shape):
    lane = lax.broadcasted_iota(jnp.int32, shape, 1)
    return jnp.where(lane < HD, first, second)


def start_of(block, me, size, count):
    return pl.multiple_of(block_place(block, me, size) * count, count)


def query_mask(info, qseg, kseg, bias, tile, count):
    me = info[0]
    for q in range(count // tile):
        rows = pl.ds(q * tile, tile)

        def fill(block, _):
            columns = pl.ds(pl.multiple_of(block * count, count), count)
            q_pos = me * count + q * tile + lax.broadcasted_iota(jnp.int32, (tile, count), 0)
            k_pos = block * count + lax.broadcasted_iota(jnp.int32, (tile, count), 1)
            seen = (k_pos <= q_pos) & (qseg[rows, 0:1] == kseg[0:1, columns])
            bias[rows, columns] = jnp.where(seen, 0.0, NEG)
            return 0

        lax.fori_loop(info[1 + q], me + 1, fill, 0)


def attend_kernel(size, tile, info, q_ref, k_ref, v_ref, qseg, kseg, out, out_low, lse, lse_row, bias):
    count = q_ref.shape[0]
    me = info[0]

    @pl.when(pl.program_id(0) == 0)
    def _():
        query_mask(info, qseg, kseg, bias, tile, count)

    for q in range(count // tile):
        rows = pl.ds(q * tile, tile)
        queries = q_ref[rows, :] * jnp.asarray(SCALE, BF16)

        def step(block, carry):
            tops, sums, total = carry
            start = start_of(block, me, size, count)
            keys = k_ref[pl.ds(start, count), :]
            values = v_ref[pl.ds(start, count), :]
            add = bias[rows, pl.ds(pl.multiple_of(block * count, count), count)]
            new_tops, new_sums, shrinks = [], [], []
            gain = jnp.zeros((tile, LANES), F32)
            for head in range(2):
                scores = dot_nt(queries, one_head(keys, head)) + add
                top = jnp.maximum(tops[head], jnp.max(scores, axis=1, keepdims=True))
                weights = jnp.exp(scores - top)
                shrink = jnp.exp(tops[head] - top)
                new_tops.append(top)
                shrinks.append(shrink)
                new_sums.append(sums[head] * shrink + jnp.sum(weights, axis=1, keepdims=True))
                gain = gain + dot_nn(weights.astype(BF16), one_head(values, head))
            total = total * per_head(shrinks[0], shrinks[1], total.shape) + gain
            return (tuple(new_tops), tuple(new_sums), total)

        column = jnp.zeros((tile, 1), F32)
        tops, sums, total = lax.fori_loop(
            info[1 + q],
            me + 1,
            step,
            ((column + NEG, column + NEG), (column, column), jnp.zeros((tile, LANES), F32)),
        )
        shape = (tile, LANES)
        result = total / per_head(sums[0], sums[1], shape)
        log_total = per_head(tops[0] + jnp.log(sums[0]), tops[1] + jnp.log(sums[1]), shape)
        out[rows, :] = result
        out_low[rows, :] = result.astype(BF16)
        lse[rows, :] = log_total
        turned = log_total.T
        lse_row[0, 0:1, rows] = turned[0:1, :]
        lse_row[0, 1:2, rows] = turned[HD : HD + 1, :]


def query_grad_kernel(size, tile, info, q_ref, k_ref, v_ref, dout, out, lse, qseg, kseg, dq, bias):
    count = q_ref.shape[0]
    me = info[0]

    @pl.when(pl.program_id(0) == 0)
    def _():
        query_mask(info, qseg, kseg, bias, tile, count)

    for q in range(count // tile):
        rows = pl.ds(q * tile, tile)
        queries = q_ref[rows, :] * jnp.asarray(SCALE, BF16)
        douts = dout[rows, :]
        both = douts.astype(F32) * out[rows, :]
        deltas = [jnp.sum(one_head(both, head), axis=1, keepdims=True) for head in range(2)]
        logs = [lse[rows, 0:1], lse[rows, HD : HD + 1]]

        def step(block, total):
            start = start_of(block, me, size, count)
            keys = k_ref[pl.ds(start, count), :]
            values = v_ref[pl.ds(start, count), :]
            add = bias[rows, pl.ds(pl.multiple_of(block * count, count), count)]
            for head in range(2):
                one_keys = one_head(keys, head)
                scores = dot_nt(queries, one_keys) + add
                probs = jnp.exp(scores - logs[head])
                prob_grad = dot_nt(douts, one_head(values, head))
                score_grad = (probs * (prob_grad - deltas[head])).astype(BF16)
                total = total + dot_nn(score_grad, one_keys)
            return total

        total = lax.fori_loop(info[1 + q], me + 1, step, jnp.zeros((tile, LANES), F32))
        dq[rows, :] = (total * SCALE).astype(BF16)


def key_grad_kernel(
    size, tile, info, k_ref, v_ref, q_ref, dout, lse_row, delta_row, kseg, qseg, dk, dv, bias
):
    count = k_ref.shape[0]
    me = info[0]
    first = 1 + count // tile

    @pl.when(pl.program_id(0) == 0)
    def _():
        for k in range(count // tile):
            rows = pl.ds(k * tile, tile)

            def fill(block, _):
                columns = pl.ds(pl.multiple_of(block * count, count), count)
                k_pos = me * count + k * tile + lax.broadcasted_iota(jnp.int32, (tile, count), 0)
                q_pos = block * count + lax.broadcasted_iota(jnp.int32, (tile, count), 1)
                seen = (k_pos <= q_pos) & (kseg[rows, 0:1] == qseg[0:1, columns])
                bias[rows, columns] = jnp.where(seen, 0.0, NEG)
                return 0

            lax.fori_loop(me, info[first + k], fill, 0)

    for k in range(count // tile):
        rows = pl.ds(k * tile, tile)
        keys = k_ref[rows, :]
        values = v_ref[rows, :]

        def step(block, carry):
            key_total, value_total = carry
            place = block_place(block, me, size)
            start = pl.multiple_of(place * count, count)
            queries = q_ref[pl.ds(start, count), :] * jnp.asarray(SCALE, BF16)
            douts = dout[pl.ds(start, count), :]
            add = bias[rows, pl.ds(pl.multiple_of(block * count, count), count)]
            for head in range(2):
                one_queries = one_head(queries, head)
                one_douts = one_head(douts, head)
                scores = dot_nt(keys, one_queries) + add
                probs = jnp.exp(scores - lse_row[place, 0, head : head + 1, :])
                prob_grad = dot_nt(values, one_douts)
                score_grad = probs * (prob_grad - delta_row[place, 0, head : head + 1, :])
                value_total = value_total + dot_nn(probs.astype(BF16), one_douts)
                key_total = key_total + dot_nn(score_grad.astype(BF16), one_queries)
            return (key_total, value_total)

        empty = jnp.zeros((tile, LANES), F32)
        key_total, value_total = lax.fori_loop(me, info[first + k], step, (empty, empty))
        dk[rows, :] = key_total.astype(BF16)
        dv[rows, :] = value_total.astype(BF16)


def strip(rows, first):
    return pl.BlockSpec((rows, LANES), lambda p, info: (0, first + p))


def whole(shape):
    return pl.BlockSpec(shape, lambda p, info: (0,) * len(shape))


def paired(count, blocks):
    if blocks is None:
        return pl.BlockSpec((1, 8, count), lambda p, info: (p, 0, 0))
    return pl.BlockSpec((blocks, 1, 8, count), lambda p, info: (0, p, 0, 0))


def call(body, in_specs, out_specs, out_shape, count, seq_len, products):
    return pl.pallas_call(
        body,
        grid_spec=pltpu.PrefetchScalarGridSpec(
            num_scalar_prefetch=1,
            grid=(PAIRS,),
            in_specs=in_specs,
            out_specs=out_specs,
            scratch_shapes=[pltpu.VMEM((count, seq_len), F32)],
        ),
        out_shape=out_shape,
        compiler_params=pltpu.CompilerParams(vmem_limit_bytes=40 * 1024 * 1024),
        cost_estimate=pl.CostEstimate(
            flops=products * 2 * count * count * 2 * 256 * H,
            bytes_accessed=8 * 1024 * 1024,
            transcendentals=count * count * H * 2,
        ),
    )


def attend(info, qkv_all, seg_col, seg_row, count, seq_len, size, tile):
    out = jax.ShapeDtypeStruct((count, D), F32)
    return call(
        functools.partial(attend_kernel, size, tile),
        [strip(count, 0), strip(seq_len, PAIRS), strip(seq_len, 2 * PAIRS), whole((count, 128)), whole((1, seq_len))],
        [strip(count, 0), strip(count, 0), strip(count, 0), paired(count, None)],
        [out, jax.ShapeDtypeStruct((count, D), BF16), out, jax.ShapeDtypeStruct((PAIRS, 8, count), F32)],
        count,
        seq_len,
        2,
    )(info, qkv_all, qkv_all, qkv_all, seg_col, seg_row)


def query_grads(info, qkv_all, dout, out, lse, seg_col, seg_row, count, seq_len, size, tile):
    return call(
        functools.partial(query_grad_kernel, size, tile),
        [strip(count, 0), strip(seq_len, PAIRS), strip(seq_len, 2 * PAIRS)]
        + [strip(count, 0)] * 3
        + [whole((count, 128)), whole((1, seq_len))],
        strip(count, 0),
        jax.ShapeDtypeStruct((count, D), BF16),
        count,
        seq_len,
        3,
    )(info, qkv_all, qkv_all, qkv_all, dout, out, lse, seg_col, seg_row)


def key_grads(info, qkv_all, dout_all, lse_row, delta_row, seg_col, seg_row, count, seq_len, size, tile):
    grad = jax.ShapeDtypeStruct((count, D), BF16)
    return call(
        functools.partial(key_grad_kernel, size, tile),
        [strip(count, PAIRS), strip(count, 2 * PAIRS), strip(seq_len, 0), strip(seq_len, 0)]
        + [paired(count, size)] * 2
        + [whole((count, 128)), whole((1, seq_len))],
        [strip(count, 0), strip(count, 0)],
        [grad, grad],
        count,
        seq_len,
        4,
    )(info, qkv_all, qkv_all, qkv_all, dout_all, lse_row, delta_row, seg_col, seg_row)


def per_device(
    reps,
    size,
    tokens,
    segment_ids,
    w_qkv,
    w_out,
    w_up,
    w_down,
    norm_gains,
    norm_shifts,
    proj_biases,
    up_bias,
    cotangent,
):
    count = tokens.shape[1]
    seq_len = segment_ids.shape[1]
    tile = min(256, count)
    me = lax.axis_index("grp")
    rep = lax.axis_index("rep")
    seg_row = segment_ids[0]
    first_row = me * count
    own_seg = lax.dynamic_slice_in_dim(seg_row, first_row, count, 0)
    seg_col = jnp.broadcast_to(own_seg[:, None], (count, 128))
    starts = own_seg[0::tile]
    ends = own_seg[tile - 1 :: tile]
    low = jnp.sum((seg_row[None, :] < starts[:, None]).astype(jnp.int32), axis=1) // count
    high = (jnp.sum((seg_row[None, :] <= ends[:, None]).astype(jnp.int32), axis=1) - 1) // count + 1
    info = jnp.concatenate([me[None].astype(jnp.int32), low, high])
    seg_row = seg_row[None]

    fetch = functools.partial(gather_weight, me=me, rep=rep, size=size, reps=reps)
    qkv_full = fetch(w_qkv)
    tokens_all = gather_near(tokens[0], size).reshape(seq_len, D)
    out_full = fetch(w_out)
    up_full = fetch(w_up)
    down_full = fetch(w_down)

    normed_all = layer_norm(tokens_all.astype(F32), norm_gains[0], norm_shifts[0]).astype(BF16)
    shift = jnp.concatenate([proj_biases[0], jnp.zeros((D,), F32), proj_biases[1]])
    qkv_all = (add_rows(normed_all, qkv_full) + shift).astype(BF16)
    normed = normed_all[:count]
    source = tokens[0].astype(F32)

    attended_f, attended, lse, lse_row = attend(
        info, qkv_all, seg_col, seg_row, count, seq_len, size, tile
    )
    middle = source + add_rows(attended, out_full) + proj_biases[2]
    second = layer_norm(middle, norm_gains[1], norm_shifts[1]).astype(BF16)
    hidden_pre = add_rows(second, up_full) + up_bias
    hidden = jax.nn.gelu(hidden_pre).astype(BF16)
    block_out = (middle + add_rows(hidden, down_full) + proj_biases[3]).astype(BF16)

    upstream = cotangent[0]
    upstream_f = upstream.astype(F32)
    total = functools.partial(total_grad, me=me, rep=rep, size=size, reps=reps)
    hidden_grad = back_rows(upstream, down_full)
    _, gelu_pull = jax.vjp(jax.nn.gelu, hidden_pre)
    pre_grad = gelu_pull(hidden_grad)[0].astype(BF16)
    second_grad = back_rows(pre_grad, up_full)
    _, second_pull = jax.vjp(layer_norm, middle, norm_gains[1], norm_shifts[1])
    middle_part, gain_second, shift_second = second_pull(second_grad)
    middle_grad = upstream_f + middle_part
    branch_grad = middle_grad.astype(BF16)
    dout = back_rows(branch_grad, out_full).astype(BF16)
    head_lanes = (
        lax.broadcasted_iota(jnp.int32, (8 * PAIRS, D), 0) // 8 * 2
        + jnp.minimum(lax.broadcasted_iota(jnp.int32, (8 * PAIRS, D), 0) % 8, 2)
    )
    lane_head = lax.broadcasted_iota(jnp.int32, (8 * PAIRS, D), 1) // HD
    minor = lax.broadcasted_iota(jnp.int32, (8 * PAIRS, D), 0) % 8
    picks = ((head_lanes == lane_head) & (minor < 2)).astype(F32)
    delta_row = jnp.einsum(
        "ed,td->et", picks, dout.astype(F32) * attended_f, precision=lax.Precision.HIGHEST
    ).reshape(PAIRS, 8, count)

    lse_rows = gather_later(lse_row, size)
    delta_rows = gather_later(delta_row, size)
    dout_all = gather_later(dout, size).reshape(seq_len, D)

    query_grad = query_grads(
        info, qkv_all, dout, attended_f, lse, seg_col, seg_row, count, seq_len, size, tile
    )
    key_grad, value_grad = key_grads(
        info, qkv_all, dout_all, lse_rows, delta_rows, seg_col, seg_row, count, seq_len, size, tile
    )
    joined_grad = jnp.concatenate([query_grad, key_grad, value_grad], axis=-1)
    normed_grad = back_rows(joined_grad, qkv_full)
    _, first_pull = jax.vjp(layer_norm, source, norm_gains[0], norm_shifts[0])
    source_part, gain_first, shift_first = first_pull(normed_grad)
    input_grad = middle_grad + source_part

    grad_down = total(hidden, upstream)
    grad_up = total(second, pre_grad)
    grad_out = total(attended, branch_grad)
    grad_qkv = total(normed, joined_grad)

    vectors = jnp.concatenate(
        [
            gain_first,
            gain_second,
            shift_first,
            shift_second,
            jnp.sum(query_grad.astype(F32), axis=0),
            jnp.sum(value_grad.astype(F32), axis=0),
            jnp.sum(branch_grad.astype(F32), axis=0),
            jnp.sum(upstream_f, axis=0),
            jnp.sum(pre_grad.astype(F32), axis=0),
        ]
    )
    vectors = total_vector(vectors.reshape(-1, 128), size, reps).reshape(-1)
    return (
        block_out[None],
        input_grad[None],
        grad_qkv,
        grad_out,
        grad_up,
        grad_down,
        vectors[: 2 * D].reshape(2, D),
        vectors[2 * D : 4 * D].reshape(2, D),
        vectors[4 * D : 8 * D].reshape(4, D),
        vectors[8 * D :],
    )


def solution(mesh):
    return jax.shard_map(
        functools.partial(per_device, mesh.shape["rep"], mesh.shape["grp"]),
        mesh=mesh,
        in_specs=(
            P("rep", "grp", None),
            P("rep", None),
            P("grp", None),
            P("grp", None),
            P("grp", None),
            P("grp", None),
            P(),
            P(),
            P(),
            P(),
            P("rep", "grp", None),
        ),
        out_specs=(
            P("rep", "grp", None),
            P("rep", "grp", None),
            P("grp", None),
            P("grp", None),
            P("grp", None),
            P("grp", None),
            P(),
            P(),
            P(),
            P(),
        ),
        check_vma=False,
    )
```

```python
import functools
import math

import jax
import jax.numpy as jnp
from jax import lax
from jax.experimental import pallas as pl
from jax.experimental.pallas import tpu as pltpu
from jax.sharding import PartitionSpec as P

D = 768
H = 12
HD = 64
FF = 3072
PAIRS = H // 2
LANES = 2 * HD
NEG = -1e30
SCALE = 1.0 / math.sqrt(HD)
F32 = jnp.float32
BF16 = jnp.bfloat16


def layer_norm(values, gain_row, shift_row):
    centre = values - jnp.mean(values, axis=-1, keepdims=True)
    spread = jnp.mean(centre * centre, axis=-1, keepdims=True)
    return centre * lax.rsqrt(spread + 1e-05) * gain_row + shift_row


def add_rows(left, piece):
    return jnp.dot(left, piece, preferred_element_type=F32)


def back_rows(right, piece):
    return jnp.einsum("te,ce->tc", right, piece, preferred_element_type=F32)


def token_product(left, right):
    return jnp.einsum("tc,te->ce", left, right, preferred_element_type=F32)


def swap(value, axis, size, mask):
    return lax.ppermute(value, axis, [(i, i ^ mask) for i in range(size)])


def bits_of(size):
    return size.bit_length() - 1


def gather_near(value, size):
    blocks = value[None]
    for bit in list(range(1, bits_of(size))) + [0]:
        blocks = jnp.concatenate([blocks, swap(blocks, "grp", size, 1 << bit)], axis=0)
    return blocks


def gather_later(value, size):
    blocks = value[None]
    for bit in list(range(1, bits_of(size))) + [0]:
        mask = 1 << bit
        if bit == 0:
            pairs = [(i, i ^ 1) for i in range(size)]
        else:
            pairs = [(i, i ^ mask) for i in range(size) if i & mask]
        blocks = jnp.concatenate([blocks, lax.ppermute(blocks, "grp", pairs)], axis=0)
    return blocks


def block_place(block, me, size):
    near = block ^ me
    return (near >> 1) | ((near & 1) << (bits_of(size) - 1))


def after(value, *others):
    return lax.optimization_barrier((value,) + others)[0]


def far_rows(weight, rep, size, reps, spread, *others):
    rows = weight.shape[0]
    side = rep & 1
    pieces = [(0, 0, weight)]
    for bit in range(1, bits_of(size)):
        mask = 1 << bit
        found = []
        for near, first, piece in pieces:
            if spread and near == 0:
                half = rows // 2
                part = lax.dynamic_slice_in_dim(piece, side * half, half, 0)
                got = swap(after(part, *others), "grp", size, mask)
                found.append((near | mask, side * half, got))
                found.append((near | mask, (1 - side) * half, swap(got, "rep", reps, 1)))
            else:
                found.append((near | mask, first, swap(after(piece, *others), "grp", size, mask)))
        pieces = pieces + found
    return pieces


def gather_weight(weight, pieces, me, size):
    rows, columns = weight.shape
    whole = jnp.zeros((size * rows, columns), weight.dtype)
    for near, first, piece in pieces:
        other = swap(piece, "grp", size, 1)
        whole = lax.dynamic_update_slice(whole, piece, ((me ^ near) * rows + first, 0))
        whole = lax.dynamic_update_slice(whole, other, ((me ^ near ^ 1) * rows + first, 0))
    return whole


def by_core(left, me, size):
    rows = left.shape[1] // size
    strips = [left[:, i * rows : (i + 1) * rows] for i in range(size)]
    even = jnp.concatenate(strips[0::2], axis=1)
    odd = jnp.concatenate(strips[1::2], axis=1)
    core = me & 1
    return jnp.where(core == 0, odd, even), jnp.where(core == 0, even, odd)


def core_grad(theirs, terms, size):
    got = swap(theirs, "grp", size, 1).astype(F32)
    mine = jnp.concatenate([token_product(left, right) for left, right in terms], axis=1)
    part = (mine + got).astype(BF16)
    return part.reshape(size // 2, -1, part.shape[1])


def other_grad(terms):
    return jnp.concatenate([token_product(left, right).astype(BF16) for left, right in terms], axis=1)


def group_step(part, bit, me, send_more=None):
    size_left, rows, columns = part.shape
    split = part.reshape(2, size_left // 2, rows, columns)
    side = (me >> bit) & 1
    send = lax.dynamic_index_in_dim(split, 1 - side, 0, keepdims=False)
    keep = lax.dynamic_index_in_dim(split, side, 0, keepdims=False)
    return send, keep


def add_low(keep, got):
    return (keep.astype(F32) + got.astype(F32)).astype(BF16)


def spread_grad(part, me, rep, size, reps, early):
    steps = [("rep", bit) for bit in early]
    steps += [("grp", bit) for bit in range(bits_of(size) - 1, 0, -1)]
    steps += [("rep", bit) for bit in range(bits_of(reps)) if bit not in early]
    undo = []
    for axis, bit in steps:
        if axis == "grp":
            send, keep = group_step(part, bit, me)
            part = add_low(keep, swap(send, "grp", size, 1 << bit))
        else:
            side = (rep >> bit) & 1
            half = part.shape[1] // 2
            send = lax.dynamic_slice_in_dim(part, (1 - side) * half, half, 1)
            keep = lax.dynamic_slice_in_dim(part, side * half, half, 1)
            part = add_low(keep, swap(send, "rep", reps, 1 << bit))
            undo.insert(0, bit)
    for bit in undo:
        side = (rep >> bit) & 1
        got = swap(part, "rep", reps, 1 << bit)
        low, high = jnp.where(side == 0, part, got), jnp.where(side == 0, got, part)
        part = jnp.concatenate([low, high], axis=1)
    return part[0].astype(F32)


def halves(vector):
    high = vector.astype(BF16)
    return jnp.concatenate([high, (vector - high.astype(F32)).astype(BF16)], axis=-2)


def from_halves(pair):
    count = pair.shape[-2] // 2
    return pair[..., :count, :].astype(F32) + pair[..., count:, :].astype(F32)


def spread_last(part, vector, me, size, reps):
    columns = part.shape[2]
    vector = vector + swap(vector, "grp", size, 1)
    for bit in range(bits_of(size) - 1, 0, -1):
        send, keep = group_step(part, bit, me)
        count = send.shape[0] * send.shape[1]
        both = jnp.concatenate([send.reshape(count, columns), halves(vector)], axis=0)
        got = swap(both, "grp", size, 1 << bit)
        part = add_low(keep, got[:count].reshape(keep.shape))
        vector = vector + from_halves(got[count:])
    pieces = part[0].reshape(reps, -1, columns)
    count = pieces.shape[1]
    extra = halves(vector)
    extra = jnp.broadcast_to(extra[None], (reps,) + extra.shape)
    got = lax.all_to_all(jnp.concatenate([pieces, extra], axis=1), "rep", 0, 0, tiled=True)
    own = jnp.sum(got[:, :count].astype(F32), axis=0).astype(BF16)
    vector = jnp.sum(from_halves(got[:, count:]), axis=0)
    every = lax.all_to_all(jnp.broadcast_to(own[None], pieces.shape), "rep", 0, 0, tiled=True)
    return every.reshape(-1, columns).astype(F32), vector


def dot_nt(left, right):
    return lax.dot_general(left, right, (((1,), (1,)), ((), ())), preferred_element_type=F32)


def dot_nn(left, right):
    return lax.dot_general(left, right, (((1,), (0,)), ((), ())), preferred_element_type=F32)


def one_head(pair, head):
    lane = lax.broadcasted_iota(jnp.int32, pair.shape, 1)
    inside = (lane < HD) if head == 0 else (lane >= HD)
    return jnp.where(inside, pair, jnp.zeros_like(pair))


def per_head(first, second, shape):
    lane = lax.broadcasted_iota(jnp.int32, shape, 1)
    return jnp.where(lane < HD, first, second)


def start_of(block, me, size, count):
    return pl.multiple_of(block_place(block, me, size) * count, count)


def query_mask(info, qseg, kseg, bias, tile, count):
    me = info[0]
    for q in range(count // tile):
        rows = pl.ds(q * tile, tile)

        def fill(block, _):
            columns = pl.ds(pl.multiple_of(block * count, count), count)
            q_pos = me * count + q * tile + lax.broadcasted_iota(jnp.int32, (tile, count), 0)
            k_pos = block * count + lax.broadcasted_iota(jnp.int32, (tile, count), 1)
            seen = (k_pos <= q_pos) & (qseg[rows, 0:1] == kseg[0:1, columns])
            bias[rows, columns] = jnp.where(seen, 0.0, NEG)
            return 0

        lax.fori_loop(info[1 + q], me + 1, fill, 0)


def attend_kernel(size, tile, info, q_ref, k_ref, v_ref, qseg, kseg, out, out_low, lse, lse_row, bias):
    count = q_ref.shape[0]
    me = info[0]

    @pl.when(pl.program_id(0) == 0)
    def _():
        query_mask(info, qseg, kseg, bias, tile, count)

    for q in range(count // tile):
        rows = pl.ds(q * tile, tile)
        queries = q_ref[rows, :] * jnp.asarray(SCALE, BF16)

        def step(block, carry):
            tops, sums, total = carry
            start = start_of(block, me, size, count)
            keys = k_ref[pl.ds(start, count), :]
            values = v_ref[pl.ds(start, count), :]
            add = bias[rows, pl.ds(pl.multiple_of(block * count, count), count)]
            new_tops, new_sums, shrinks = [], [], []
            gain = jnp.zeros((tile, LANES), F32)
            for head in range(2):
                scores = dot_nt(queries, one_head(keys, head)) + add
                top = jnp.maximum(tops[head], jnp.max(scores, axis=1, keepdims=True))
                weights = jnp.exp(scores - top)
                shrink = jnp.exp(tops[head] - top)
                new_tops.append(top)
                shrinks.append(shrink)
                new_sums.append(sums[head] * shrink + jnp.sum(weights, axis=1, keepdims=True))
                gain = gain + dot_nn(weights.astype(BF16), one_head(values, head))
            total = total * per_head(shrinks[0], shrinks[1], total.shape) + gain
            return (tuple(new_tops), tuple(new_sums), total)

        column = jnp.zeros((tile, 1), F32)
        tops, sums, total = lax.fori_loop(
            info[1 + q],
            me + 1,
            step,
            ((column + NEG, column + NEG), (column, column), jnp.zeros((tile, LANES), F32)),
        )
        shape = (tile, LANES)
        result = total / per_head(sums[0], sums[1], shape)
        log_total = per_head(tops[0] + jnp.log(sums[0]), tops[1] + jnp.log(sums[1]), shape)
        out[rows, :] = result
        out_low[rows, :] = result.astype(BF16)
        lse[rows, :] = log_total
        turned = log_total.T
        lse_row[0, :, rows] = jnp.zeros((8, tile), F32)
        lse_row[0, 0:1, rows] = turned[0:1, :]
        lse_row[0, 1:2, rows] = turned[HD : HD + 1, :]


def query_grad_kernel(size, tile, info, q_ref, k_ref, v_ref, dout, out, lse, qseg, kseg, dq, bias):
    count = q_ref.shape[0]
    me = info[0]

    @pl.when(pl.program_id(0) == 0)
    def _():
        query_mask(info, qseg, kseg, bias, tile, count)

    for q in range(count // tile):
        rows = pl.ds(q * tile, tile)
        queries = q_ref[rows, :] * jnp.asarray(SCALE, BF16)
        douts = dout[rows, :]
        both = douts.astype(F32) * out[rows, :]
        deltas = [jnp.sum(one_head(both, head), axis=1, keepdims=True) for head in range(2)]
        logs = [lse[rows, 0:1], lse[rows, HD : HD + 1]]

        def step(block, total):
            start = start_of(block, me, size, count)
            keys = k_ref[pl.ds(start, count), :]
            values = v_ref[pl.ds(start, count), :]
            add = bias[rows, pl.ds(pl.multiple_of(block * count, count), count)]
            for head in range(2):
                one_keys = one_head(keys, head)
                scores = dot_nt(queries, one_keys) + add
                probs = jnp.exp(scores - logs[head])
                prob_grad = dot_nt(douts, one_head(values, head))
                score_grad = (probs * (prob_grad - deltas[head])).astype(BF16)
                total = total + dot_nn(score_grad, one_keys)
            return total

        total = lax.fori_loop(info[1 + q], me + 1, step, jnp.zeros((tile, LANES), F32))
        dq[rows, :] = (total * SCALE).astype(BF16)


def key_grad_kernel(
    size, tile, info, k_ref, v_ref, q_ref, dout, stats, kseg, qseg, dk, dv, bias
):
    count = k_ref.shape[0]
    me = info[0]
    first = 1 + count // tile

    @pl.when(pl.program_id(0) == 0)
    def _():
        for k in range(count // tile):
            rows = pl.ds(k * tile, tile)

            def fill(block, _):
                columns = pl.ds(pl.multiple_of(block * count, count), count)
                k_pos = me * count + k * tile + lax.broadcasted_iota(jnp.int32, (tile, count), 0)
                q_pos = block * count + lax.broadcasted_iota(jnp.int32, (tile, count), 1)
                seen = (k_pos <= q_pos) & (kseg[rows, 0:1] == qseg[0:1, columns])
                bias[rows, columns] = jnp.where(seen, 0.0, NEG)
                return 0

            lax.fori_loop(me, info[first + k], fill, 0)

    for k in range(count // tile):
        rows = pl.ds(k * tile, tile)
        keys = k_ref[rows, :]
        values = v_ref[rows, :]

        def step(block, carry):
            key_total, value_total = carry
            place = block_place(block, me, size)
            start = pl.multiple_of(place * count, count)
            queries = q_ref[pl.ds(start, count), :] * jnp.asarray(SCALE, BF16)
            douts = dout[pl.ds(start, count), :]
            add = bias[rows, pl.ds(pl.multiple_of(block * count, count), count)]
            for head in range(2):
                one_queries = one_head(queries, head)
                one_douts = one_head(douts, head)
                scores = dot_nt(keys, one_queries) + add
                probs = jnp.exp(scores - stats[place, 0, head : head + 1, :])
                prob_grad = dot_nt(values, one_douts)
                score_grad = probs * (prob_grad - stats[place, 0, 2 + head : 3 + head, :])
                value_total = value_total + dot_nn(probs.astype(BF16), one_douts)
                key_total = key_total + dot_nn(score_grad.astype(BF16), one_queries)
            return (key_total, value_total)

        empty = jnp.zeros((tile, LANES), F32)
        key_total, value_total = lax.fori_loop(me, info[first + k], step, (empty, empty))
        dk[rows, :] = key_total.astype(BF16)
        dv[rows, :] = value_total.astype(BF16)


def strip(rows, first):
    return pl.BlockSpec((rows, LANES), lambda p, info: (0, first + p))


def whole(shape):
    return pl.BlockSpec(shape, lambda p, info: (0,) * len(shape))


def paired(count, blocks, first=0):
    if blocks is None:
        return pl.BlockSpec((1, 8, count), lambda p, info: (p, 0, 0))
    return pl.BlockSpec((blocks, 1, 8, count), lambda p, info: (0, first + p, 0, 0))


def call(body, in_specs, out_specs, out_shape, count, seq_len, products, pairs):
    return pl.pallas_call(
        body,
        grid_spec=pltpu.PrefetchScalarGridSpec(
            num_scalar_prefetch=1,
            grid=(pairs,),
            in_specs=in_specs,
            out_specs=out_specs,
            scratch_shapes=[pltpu.VMEM((count, seq_len), F32)],
        ),
        out_shape=out_shape,
        compiler_params=pltpu.CompilerParams(vmem_limit_bytes=40 * 1024 * 1024),
        cost_estimate=pl.CostEstimate(
            flops=products * 2 * count * count * 2 * 256 * 2 * pairs,
            bytes_accessed=8 * 1024 * 1024,
            transcendentals=count * count * 4 * pairs,
        ),
    )


def attend(info, qkv_all, seg_col, seg_row, count, seq_len, size, tile):
    out = jax.ShapeDtypeStruct((count, D), F32)
    return call(
        functools.partial(attend_kernel, size, tile),
        [strip(count, 0), strip(seq_len, PAIRS), strip(seq_len, 2 * PAIRS), whole((count, 128)), whole((1, seq_len))],
        [strip(count, 0), strip(count, 0), strip(count, 0), paired(count, None)],
        [out, jax.ShapeDtypeStruct((count, D), BF16), out, jax.ShapeDtypeStruct((PAIRS, 8, count), F32)],
        count,
        seq_len,
        2,
        PAIRS,
    )(info, qkv_all, qkv_all, qkv_all, seg_col, seg_row)


def query_grads(first, pairs, info, qkv_all, dout, out, lse, seg_col, seg_row, count, seq_len, size, tile):
    return call(
        functools.partial(query_grad_kernel, size, tile),
        [strip(count, first), strip(seq_len, PAIRS + first), strip(seq_len, 2 * PAIRS + first)]
        + [strip(count, first)] * 3
        + [whole((count, 128)), whole((1, seq_len))],
        strip(count, 0),
        jax.ShapeDtypeStruct((count, pairs * LANES), BF16),
        count,
        seq_len,
        3,
        pairs,
    )(info, qkv_all, qkv_all, qkv_all, dout, out, lse, seg_col, seg_row)


def key_grads(first, pairs, info, qkv_all, dout_all, stats, seg_col, seg_row, count, seq_len, size, tile):
    grad = jax.ShapeDtypeStruct((count, pairs * LANES), BF16)
    return call(
        functools.partial(key_grad_kernel, size, tile),
        [strip(count, PAIRS + first), strip(count, 2 * PAIRS + first), strip(seq_len, first), strip(seq_len, first)]
        + [paired(count, size, first)]
        + [whole((count, 128)), whole((1, seq_len))],
        [strip(count, 0), strip(count, 0)],
        [grad, grad],
        count,
        seq_len,
        4,
        pairs,
    )(info, qkv_all, qkv_all, qkv_all, dout_all, stats, seg_col, seg_row)


def per_device(
    reps,
    size,
    tokens,
    segment_ids,
    w_qkv,
    w_out,
    w_up,
    w_down,
    norm_gains,
    norm_shifts,
    proj_biases,
    up_bias,
    cotangent,
):
    count = tokens.shape[1]
    seq_len = segment_ids.shape[1]
    tile = min(256, count)
    me = lax.axis_index("grp")
    rep = lax.axis_index("rep")
    seg_row = segment_ids[0]
    first_row = me * count
    own_seg = lax.dynamic_slice_in_dim(seg_row, first_row, count, 0)
    seg_col = jnp.broadcast_to(own_seg[:, None], (count, 128))
    starts = own_seg[0::tile]
    ends = own_seg[tile - 1 :: tile]
    low = jnp.sum((seg_row[None, :] < starts[:, None]).astype(jnp.int32), axis=1) // count
    high = (jnp.sum((seg_row[None, :] <= ends[:, None]).astype(jnp.int32), axis=1) - 1) // count + 1
    info = jnp.concatenate([me[None].astype(jnp.int32), low, high])
    seg_row = seg_row[None]

    near_qkv = far_rows(w_qkv, rep, size, reps, True)
    tokens_all = gather_near(tokens[0], size).reshape(seq_len, D)
    first_far = near_qkv[1][2]
    near_out = far_rows(w_out, rep, size, reps, False, first_far)
    near_up = far_rows(w_up, rep, size, reps, True, first_far)
    near_down = far_rows(w_down, rep, size, reps, True, near_up[1][2])
    qkv_full = gather_weight(w_qkv, near_qkv, me, size)
    out_full = gather_weight(w_out, near_out, me, size)
    up_full = gather_weight(w_up, near_up, me, size)
    down_full = gather_weight(w_down, near_down, me, size)

    normed_all = layer_norm(tokens_all.astype(F32), norm_gains[0], norm_shifts[0]).astype(BF16)
    shift = jnp.concatenate([proj_biases[0], jnp.zeros((D,), F32), proj_biases[1]])
    qkv_all = (add_rows(normed_all, qkv_full) + shift).astype(BF16)
    normed = normed_all[:count]
    source = tokens[0].astype(F32)

    attended_f, attended, lse, lse_row = attend(
        info, qkv_all, seg_col, seg_row, count, seq_len, size, tile
    )
    middle = source + add_rows(attended, out_full) + proj_biases[2]
    second = layer_norm(middle, norm_gains[1], norm_shifts[1]).astype(BF16)
    hidden_pre = add_rows(second, up_full) + up_bias
    hidden = jax.nn.gelu(hidden_pre).astype(BF16)

    upstream = cotangent[0]
    upstream_f = upstream.astype(F32)
    hidden_theirs, hidden_mine = by_core(hidden, me, size)
    down_theirs = other_grad([(hidden_theirs, upstream)])
    hidden_grad = back_rows(after(upstream, down_theirs), down_full)
    _, gelu_pull = jax.vjp(jax.nn.gelu, hidden_pre)
    pre_grad = gelu_pull(hidden_grad)[0].astype(BF16)
    down_part = core_grad(down_theirs, [(after(hidden_mine, pre_grad), upstream)], size)
    second_grad = back_rows(after(pre_grad, down_part), up_full)
    _, second_pull = jax.vjp(layer_norm, middle, norm_gains[1], norm_shifts[1])
    middle_part, gain_second, shift_second = second_pull(second_grad)
    middle_grad = upstream_f + middle_part
    branch_grad = middle_grad.astype(BF16)
    dout = back_rows(branch_grad, out_full).astype(BF16)
    row = lax.broadcasted_iota(jnp.int32, (8 * PAIRS, D), 0)
    minor = row % 8 - 2
    lane_head = lax.broadcasted_iota(jnp.int32, (8 * PAIRS, D), 1) // HD
    picks = ((row // 8 * 2 + minor == lane_head) & (minor >= 0) & (minor < 2)).astype(F32)
    delta_row = jnp.einsum(
        "ed,td->et", picks, dout.astype(F32) * attended_f, precision=lax.Precision.HIGHEST
    ).reshape(PAIRS, 8, count)
    stats = gather_later(lse_row + delta_row, size)
    dout_all = gather_later(dout, size).reshape(seq_len, D)

    second_theirs, second_mine = by_core(second, me, size)
    attended_theirs, attended_mine = by_core(attended, me, size)
    up_theirs = other_grad([(second_theirs, after(pre_grad, dout)), (attended_theirs, after(branch_grad, dout))])
    up_part = core_grad(up_theirs, [(second_mine, pre_grad), (attended_mine, branch_grad)], size)
    grad_down = spread_grad(down_part, me, rep, size, reps, (0,))
    grad_up_out = spread_grad(up_part, me, rep, size, reps, ())

    part = PAIRS // 2
    queries_one = query_grads(
        0, part, info, qkv_all, dout, attended_f, lse, seg_col, seg_row, count, seq_len, size, tile
    )
    queries_two = query_grads(
        part, part, info, qkv_all, after(dout, queries_one, up_part), attended_f, lse, seg_col, seg_row, count, seq_len, size, tile
    )
    keys_one, values_one = key_grads(
        0, part, info, qkv_all, after(dout_all, queries_two), stats, seg_col, seg_row, count, seq_len, size, tile
    )
    normed_theirs, normed_mine = by_core(normed, me, size)
    first_joined = jnp.concatenate([queries_one, queries_two, keys_one, values_one], axis=1)
    first_theirs = other_grad([(normed_theirs, first_joined)])
    keys_two, values_two = key_grads(
        part, part, info, qkv_all, after(dout_all, first_theirs), stats, seg_col, seg_row, count, seq_len, size, tile
    )
    first_part = core_grad(first_theirs, [(normed_mine, first_joined)], size)
    grad_first = spread_grad(first_part, me, rep, size, reps, ())
    last_joined = jnp.concatenate([keys_two, values_two], axis=1)
    last_theirs = other_grad([(normed_theirs, last_joined)])
    last_part = core_grad(last_theirs, [(normed_mine, last_joined)], size)

    joined_grad = jnp.concatenate(
        [queries_one, queries_two, keys_one, keys_two, values_one, values_two], axis=-1
    )
    normed_grad = back_rows(joined_grad, qkv_full)
    _, first_pull = jax.vjp(layer_norm, source, norm_gains[0], norm_shifts[0])
    source_part, gain_first, shift_first = first_pull(normed_grad)
    input_grad = middle_grad + source_part
    block_out = (middle + add_rows(hidden, down_full) + proj_biases[3]).astype(BF16)

    vectors = jnp.concatenate(
        [
            gain_first,
            gain_second,
            shift_first,
            shift_second,
            jnp.sum(joined_grad[:, :D].astype(F32), axis=0),
            jnp.sum(joined_grad[:, 2 * D :].astype(F32), axis=0),
            jnp.sum(branch_grad.astype(F32), axis=0),
            jnp.sum(upstream_f, axis=0),
            jnp.sum(pre_grad.astype(F32), axis=0),
        ]
    )
    grad_last, vectors = spread_last(last_part, vectors.reshape(-1, last_part.shape[2]), me, size, reps)
    vectors = vectors.reshape(-1)
    half = D // 2
    grad_qkv = jnp.concatenate(
        [grad_first[:, : D + half], grad_last[:, :half], grad_first[:, D + half :], grad_last[:, half:]], axis=1
    )
    grad_up, grad_out = grad_up_out[:, :FF], grad_up_out[:, FF:]
    return (
        block_out[None],
        input_grad[None],
        grad_qkv,
        grad_out,
        grad_up,
        grad_down,
        vectors[: 2 * D].reshape(2, D),
        vectors[2 * D : 4 * D].reshape(2, D),
        vectors[4 * D : 8 * D].reshape(4, D),
        vectors[8 * D :],
    )


def solution(mesh):
    return jax.shard_map(
        functools.partial(per_device, mesh.shape["rep"], mesh.shape["grp"]),
        mesh=mesh,
        in_specs=(
            P("rep", "grp", None),
            P("rep", None),
            P("grp", None),
            P("grp", None),
            P("grp", None),
            P("grp", None),
            P(),
            P(),
            P(),
            P(),
            P("rep", "grp", None),
        ),
        out_specs=(
            P("rep", "grp", None),
            P("rep", "grp", None),
            P("grp", None),
            P("grp", None),
            P("grp", None),
            P("grp", None),
            P(),
            P(),
            P(),
            P(),
        ),
        check_vma=False,
    )
```

```python
import functools
import math

import jax
import jax.numpy as jnp
from jax import lax
from jax.experimental import pallas as pl
from jax.experimental.pallas import tpu as pltpu
from jax.sharding import PartitionSpec as P

D = 768
H = 12
HD = 64
FF = 3072
PAIRS = H // 2
LANES = 2 * HD
NEG = -1e30
SCALE = 1.0 / math.sqrt(HD)
F32 = jnp.float32
BF16 = jnp.bfloat16


def layer_norm(values, gain_row, shift_row):
    centre = values - jnp.mean(values, axis=-1, keepdims=True)
    spread = jnp.mean(centre * centre, axis=-1, keepdims=True)
    return centre * lax.rsqrt(spread + 1e-05) * gain_row + shift_row


def add_rows(left, piece):
    return jnp.dot(left, piece, preferred_element_type=F32)


def back_rows(right, piece):
    return jnp.einsum("te,ce->tc", right, piece, preferred_element_type=F32)


def token_product(left, right):
    return jnp.einsum("tc,te->ce", left, right, preferred_element_type=F32)


def after(value, *others):
    return lax.optimization_barrier((value,) + others)[0]


def swap(value, axis, size, mask, *until):
    got = lax.ppermute(value, axis, [(i, i ^ mask) for i in range(size)])
    return after(got, *until) if until else got


def bits_of(size):
    return size.bit_length() - 1


def gather_later(value, size, *until):
    blocks = value[None]
    for bit in list(range(1, bits_of(size))) + [0]:
        mask = 1 << bit
        if bit == 0:
            pairs = [(i, i ^ 1) for i in range(size)]
        else:
            pairs = [(i, i ^ mask) for i in range(size) if i & mask]
        got = after(lax.ppermute(blocks, "grp", pairs), until[0] if bit else until[1])
        blocks = jnp.concatenate([blocks, got], axis=0)
    return blocks


def block_place(block, me, size):
    near = block ^ me
    return (near >> 1) | ((near & 1) << (bits_of(size) - 1))


def far_rows(weight, rep, size, reps, spread, before, y_until, x_until):
    rows = weight.shape[0]
    side = rep & 1
    half = rows // 2
    spread = spread and half % 16 == 0
    pieces = [(0, 0, weight)]
    for bit in range(1, bits_of(size)):
        mask = 1 << bit
        found = []
        for near, first, piece in pieces:
            if spread and near == 0:
                part = lax.dynamic_slice_in_dim(piece, side * half, half, 0)
                got = swap(after(part, *before), "grp", size, mask, *y_until)
                found.append((near | mask, side * half, got))
                found.append((near | mask, (1 - side) * half, swap(got, "rep", reps, 1, *x_until)))
            else:
                found.append((near | mask, first, swap(after(piece, *before), "grp", size, mask, *y_until)))
        pieces = pieces + found
    return pieces


def both_cores(pieces, own_other, size, me, rows, until=()):
    starts, found = [], []
    for near, first, piece in pieces:
        starts += [(me ^ near) * rows + first, (me ^ near ^ 1) * rows + first]
        other = own_other if near == 0 else swap(piece, "grp", size, 1, *until)
        found += [piece, other]
    return starts, found


def place_kernel(counts, starts, *refs):
    pieces, (out, sem) = refs[:-2], refs[-2:]
    copies = []
    for i, count in enumerate(counts):
        start = pl.multiple_of(starts[i] * 16, 16)
        copies.append(pltpu.make_async_copy(pieces[i], out.at[pl.ds(start, count), :], sem.at[i]))
    for copy in copies:
        copy.start()
    for copy in copies:
        copy.wait()


def place_rows(weight, size, starts, pieces):
    rows, columns = weight.shape
    counts = [piece.shape[0] for piece in pieces]
    anywhere = pl.BlockSpec(memory_space=pl.ANY)
    return pl.pallas_call(
        functools.partial(place_kernel, counts),
        grid_spec=pltpu.PrefetchScalarGridSpec(
            num_scalar_prefetch=1,
            grid=(1,),
            in_specs=[anywhere] * len(pieces),
            out_specs=pl.BlockSpec((size * rows, columns), lambda i, starts: (0, 0)),
            scratch_shapes=[pltpu.SemaphoreType.DMA((len(pieces),))],
        ),
        out_shape=jax.ShapeDtypeStruct((size * rows, columns), weight.dtype),
        compiler_params=pltpu.CompilerParams(vmem_limit_bytes=40 * 1024 * 1024),
        cost_estimate=pl.CostEstimate(
            flops=0, bytes_accessed=4 * size * rows * columns, transcendentals=0
        ),
    )(jnp.stack(starts).astype(jnp.int32) // 16, *pieces)


def by_core(left, me, size):
    rows = left.shape[1] // size
    core = me & 1
    if rows % 128 == 0:
        return [
            jnp.concatenate(
                [lax.dynamic_slice_in_dim(left, (2 * i + which) * rows, rows, 1) for i in range(size // 2)], axis=1
            )
            for which in (1 - core, core)
        ]
    strips = [left[:, i * rows : (i + 1) * rows] for i in range(size)]
    even = jnp.concatenate(strips[0::2], axis=1)
    odd = jnp.concatenate(strips[1::2], axis=1)
    return jnp.where(core == 0, odd, even), jnp.where(core == 0, even, odd)


def group_step(part, bit, me):
    size_left, rows, columns = part.shape
    split = part.reshape(2, size_left // 2, rows, columns)
    side = (me >> bit) & 1
    send = lax.dynamic_index_in_dim(split, 1 - side, 0, keepdims=False)
    keep = lax.dynamic_index_in_dim(split, side, 0, keepdims=False)
    return send, keep


def group_sum(part, me, size, *until):
    for bit in range(bits_of(part.shape[0]), 0, -1):
        send, keep = group_step(part, bit, me)
        part = add_low(keep, swap(send, "grp", size, 1 << bit, *until))
    return part


def add_low(keep, got):
    return (keep.astype(F32) + got.astype(F32)).astype(BF16)


def rep_halves(part, rep):
    axis = part.ndim - 2
    half = part.shape[axis] // 2
    side = rep & 1
    send = lax.dynamic_slice_in_dim(part, (1 - side) * half, half, axis)
    keep = lax.dynamic_slice_in_dim(part, side * half, half, axis)
    return send, keep


def scatter_far(part, rep, reps, *until):
    count = reps // 2
    place = rep >> 1
    pieces = part.reshape(count, -1, part.shape[1])
    total = lax.dynamic_index_in_dim(pieces, place, 0, keepdims=False).astype(F32)
    for mask in range(1, count):
        send = lax.dynamic_index_in_dim(pieces, place ^ mask, 0, keepdims=False)
        total = total + swap(send, "rep", reps, mask << 1, *until).astype(F32)
    return total.astype(BF16)


def share_far(own, rep, reps, *until):
    count = reps // 2
    place = rep >> 1
    near = [own] + [swap(own, "rep", reps, mask << 1, *until) for mask in range(1, count)]
    ordered = []
    for i in range(count):
        value = near[i]
        for j in range(1, count):
            value = jnp.where(place == j, near[i ^ j], value)
        ordered.append(value)
    return jnp.concatenate(ordered, axis=0)


def as_rows(part):
    return jnp.concatenate([part[:, i : i + D] for i in range(0, part.shape[1], D)], axis=0)


def in_order(own, got, rep):
    side = rep & 1
    low, high = jnp.where(side == 0, own, got), jnp.where(side == 0, got, own)
    return jnp.concatenate([low, high], axis=0)


def total_vector(value, size, reps, pace):
    steps = [("grp", bit) for bit in range(bits_of(size))] + [("rep", bit) for bit in range(bits_of(reps))]
    for i, (axis, bit) in enumerate(steps):
        count = size if axis == "grp" else reps
        value = value + swap(value, axis, count, 1 << bit, pace[min(i, len(pace) - 1)])
    return value


def other_grad(left, right):
    return token_product(left, right).astype(BF16)


def core_grad(theirs, left, right, size, *until):
    got = swap(theirs, "grp", size, 1, *until).astype(F32)
    part = (token_product(left, right) + got).astype(BF16)
    return part.reshape(size // 2, -1, part.shape[1])


def dot_nt(left, right):
    return lax.dot_general(left, right, (((1,), (1,)), ((), ())), preferred_element_type=F32)


def dot_nn(left, right):
    return lax.dot_general(left, right, (((1,), (0,)), ((), ())), preferred_element_type=F32)


def one_head(pair, head):
    lane = lax.broadcasted_iota(jnp.int32, pair.shape, 1)
    inside = (lane < HD) if head == 0 else (lane >= HD)
    return jnp.where(inside, pair, jnp.zeros_like(pair))


def per_head(first, second, shape):
    lane = lax.broadcasted_iota(jnp.int32, shape, 1)
    return jnp.where(lane < HD, first, second)


def start_of(block, me, size, count):
    return pl.multiple_of(block_place(block, me, size) * count, count)


def query_mask(info, qseg, kseg, bias, tile, count):
    me = info[0]
    for q in range(count // tile):
        rows = pl.ds(q * tile, tile)

        def fill(block, _):
            columns = pl.ds(pl.multiple_of(block * count, count), count)
            q_pos = me * count + q * tile + lax.broadcasted_iota(jnp.int32, (tile, count), 0)
            k_pos = block * count + lax.broadcasted_iota(jnp.int32, (tile, count), 1)
            seen = (k_pos <= q_pos) & (qseg[rows, 0:1] == kseg[0:1, columns])
            bias[rows, columns] = jnp.where(seen, 0.0, NEG)
            return 0

        lax.fori_loop(info[1 + q], me + 1, fill, 0)


def attend_kernel(size, tile, skip, info, q_ref, k_ref, v_ref, qseg, kseg, *refs):
    out, out_low, lse, lse_row, bias = refs[skip:]
    count = q_ref.shape[0]
    me = info[0]

    @pl.when(pl.program_id(0) == 0)
    def _():
        query_mask(info, qseg, kseg, bias, tile, count)

    for q in range(count // tile):
        rows = pl.ds(q * tile, tile)
        queries = q_ref[rows, :] * jnp.asarray(SCALE, BF16)

        def step(block, carry):
            tops, sums, total = carry
            start = start_of(block, me, size, count)
            keys = k_ref[pl.ds(start, count), :]
            values = v_ref[pl.ds(start, count), :]
            add = bias[rows, pl.ds(pl.multiple_of(block * count, count), count)]
            new_tops, new_sums, shrinks = [], [], []
            gain = jnp.zeros((tile, LANES), F32)
            for head in range(2):
                scores = dot_nt(queries, one_head(keys, head)) + add
                top = jnp.maximum(tops[head], jnp.max(scores, axis=1, keepdims=True))
                weights = jnp.exp(scores - top)
                shrink = jnp.exp(tops[head] - top)
                new_tops.append(top)
                shrinks.append(shrink)
                new_sums.append(sums[head] * shrink + jnp.sum(weights, axis=1, keepdims=True))
                gain = gain + dot_nn(weights.astype(BF16), one_head(values, head))
            total = total * per_head(shrinks[0], shrinks[1], total.shape) + gain
            return (tuple(new_tops), tuple(new_sums), total)

        column = jnp.zeros((tile, 1), F32)
        tops, sums, total = lax.fori_loop(
            info[1 + q],
            me + 1,
            step,
            ((column + NEG, column + NEG), (column, column), jnp.zeros((tile, LANES), F32)),
        )
        shape = (tile, LANES)
        result = total / per_head(sums[0], sums[1], shape)
        log_total = per_head(tops[0] + jnp.log(sums[0]), tops[1] + jnp.log(sums[1]), shape)
        out[rows, :] = result
        out_low[rows, :] = result.astype(BF16)
        lse[rows, :] = log_total
        turned = log_total.T
        lse_row[0, :, rows] = jnp.zeros((8, tile), F32)
        lse_row[0, 0:1, rows] = turned[0:1, :]
        lse_row[0, 1:2, rows] = turned[HD : HD + 1, :]


def query_grad_kernel(size, tile, info, q_ref, k_ref, v_ref, dout, out, lse, qseg, kseg, dq, bias):
    count = q_ref.shape[0]
    me = info[0]

    @pl.when(pl.program_id(0) == 0)
    def _():
        query_mask(info, qseg, kseg, bias, tile, count)

    for q in range(count // tile):
        rows = pl.ds(q * tile, tile)
        queries = q_ref[rows, :] * jnp.asarray(SCALE, BF16)
        douts = dout[rows, :]
        both = douts.astype(F32) * out[rows, :]
        deltas = [jnp.sum(one_head(both, head), axis=1, keepdims=True) for head in range(2)]
        logs = [lse[rows, 0:1], lse[rows, HD : HD + 1]]

        def step(block, total):
            start = start_of(block, me, size, count)
            keys = k_ref[pl.ds(start, count), :]
            values = v_ref[pl.ds(start, count), :]
            add = bias[rows, pl.ds(pl.multiple_of(block * count, count), count)]
            for head in range(2):
                one_keys = one_head(keys, head)
                scores = dot_nt(queries, one_keys) + add
                probs = jnp.exp(scores - logs[head])
                prob_grad = dot_nt(douts, one_head(values, head))
                score_grad = (probs * (prob_grad - deltas[head])).astype(BF16)
                total = total + dot_nn(score_grad, one_keys)
            return total

        total = lax.fori_loop(info[1 + q], me + 1, step, jnp.zeros((tile, LANES), F32))
        dq[rows, :] = (total * SCALE).astype(BF16)


def key_grad_kernel(
    size, tile, info, k_ref, v_ref, q_ref, dout, stats, kseg, qseg, dkv, bias
):
    count = k_ref.shape[0]
    me = info[0]
    first = 1 + count // tile

    @pl.when(pl.program_id(0) == 0)
    def _():
        for k in range(count // tile):
            rows = pl.ds(k * tile, tile)

            def fill(block, _):
                columns = pl.ds(pl.multiple_of(block * count, count), count)
                k_pos = me * count + k * tile + lax.broadcasted_iota(jnp.int32, (tile, count), 0)
                q_pos = block * count + lax.broadcasted_iota(jnp.int32, (tile, count), 1)
                seen = (k_pos <= q_pos) & (kseg[rows, 0:1] == qseg[0:1, columns])
                bias[rows, columns] = jnp.where(seen, 0.0, NEG)
                return 0

            lax.fori_loop(me, info[first + k], fill, 0)

    for k in range(count // tile):
        rows = pl.ds(k * tile, tile)
        keys = k_ref[rows, :]
        values = v_ref[rows, :]

        def step(block, carry):
            key_total, value_total = carry
            place = block_place(block, me, size)
            start = pl.multiple_of(place * count, count)
            queries = q_ref[pl.ds(start, count), :] * jnp.asarray(SCALE, BF16)
            douts = dout[pl.ds(start, count), :]
            add = bias[rows, pl.ds(pl.multiple_of(block * count, count), count)]
            for head in range(2):
                one_queries = one_head(queries, head)
                one_douts = one_head(douts, head)
                scores = dot_nt(keys, one_queries) + add
                probs = jnp.exp(scores - stats[place, 0, head : head + 1, :])
                prob_grad = dot_nt(values, one_douts)
                score_grad = probs * (prob_grad - stats[place, 0, 2 + head : 3 + head, :])
                value_total = value_total + dot_nn(probs.astype(BF16), one_douts)
                key_total = key_total + dot_nn(score_grad.astype(BF16), one_queries)
            return (key_total, value_total)

        empty = jnp.zeros((tile, LANES), F32)
        key_total, value_total = lax.fori_loop(me, info[first + k], step, (empty, empty))
        dkv[rows, :LANES] = key_total.astype(BF16)
        dkv[rows, LANES:] = value_total.astype(BF16)


def strip(rows, first, stride=1):
    return pl.BlockSpec((rows, LANES), lambda p, info: (0, first + stride * p))


def whole(shape):
    return pl.BlockSpec(shape, lambda p, info: (0,) * len(shape))


def paired(count, blocks, first=0):
    if blocks is None:
        return pl.BlockSpec((1, 8, count), lambda p, info: (first + p, 0, 0))
    return pl.BlockSpec((blocks, 1, 8, count), lambda p, info: (0, first + p, 0, 0))


def call(body, in_specs, out_specs, out_shape, count, seq_len, products, pairs, mib=60, aliases=None):
    return pl.pallas_call(
        body,
        grid_spec=pltpu.PrefetchScalarGridSpec(
            num_scalar_prefetch=1,
            grid=(pairs,),
            in_specs=in_specs,
            out_specs=out_specs,
            scratch_shapes=[pltpu.VMEM((count, seq_len), F32)],
        ),
        out_shape=out_shape,
        input_output_aliases=aliases or {},
        compiler_params=pltpu.CompilerParams(vmem_limit_bytes=mib * 1024 * 1024),
        cost_estimate=pl.CostEstimate(
            flops=products * 2 * count * count * 2 * 256 * 2 * pairs,
            bytes_accessed=8 * 1024 * 1024,
            transcendentals=count * count * 4 * pairs,
        ),
    )


def key_value_strips(rows, first):
    return [strip(rows, PAIRS + 2 * first, 2), strip(rows, PAIRS + 2 * first + 1, 2)]


def attend(first, pairs, info, qkv_all, earlier, seg_col, seg_row, count, seq_len, size, tile):
    out = jax.ShapeDtypeStruct((count, D), F32)
    return call(
        functools.partial(attend_kernel, size, tile, len(earlier)),
        [strip(count, first)]
        + key_value_strips(seq_len, first)
        + [whole((count, 128)), whole((1, seq_len))]
        + [pl.BlockSpec(memory_space=pl.ANY)] * len(earlier),
        [strip(count, first), strip(count, first), strip(count, first), paired(count, None, first)],
        [out, jax.ShapeDtypeStruct((count, D), BF16), out, jax.ShapeDtypeStruct((PAIRS, 8, count), F32)],
        count,
        seq_len,
        2,
        pairs,
        40,
        {6 + i: i for i in range(len(earlier))},
    )(info, qkv_all, qkv_all, qkv_all, seg_col, seg_row, *earlier)


def query_grads(first, pairs, info, qkv_all, dout, out, lse, seg_col, seg_row, count, seq_len, size, tile):
    return call(
        functools.partial(query_grad_kernel, size, tile),
        [strip(count, first)] + key_value_strips(seq_len, first)
        + [strip(count, first)] * 3
        + [whole((count, 128)), whole((1, seq_len))],
        strip(count, 0),
        jax.ShapeDtypeStruct((count, pairs * LANES), BF16),
        count,
        seq_len,
        3,
        pairs,
    )(info, qkv_all, qkv_all, qkv_all, dout, out, lse, seg_col, seg_row)


def key_grads(first, pairs, info, qkv_all, dout_all, stats, seg_col, seg_row, count, seq_len, size, tile):
    return call(
        functools.partial(key_grad_kernel, size, tile),
        key_value_strips(count, first) + [strip(seq_len, first)] * 2
        + [paired(count, size, first)]
        + [whole((count, 128)), whole((1, seq_len))],
        pl.BlockSpec((count, 2 * LANES), lambda p, info: (0, p)),
        jax.ShapeDtypeStruct((count, pairs * 2 * LANES), BF16),
        count,
        seq_len,
        4,
        pairs,
    )(info, qkv_all, qkv_all, qkv_all, dout_all, stats, seg_col, seg_row)


def key_value_mixed(columns):
    rows = columns.shape[0]
    pairs = columns.reshape(rows, 2, PAIRS, LANES)
    return jnp.concatenate([pairs[:, i % 2, i // 2] for i in range(2 * PAIRS)], axis=1)


def key_value_apart(columns):
    rows, width = columns.shape
    strips = [columns[:, i * LANES : (i + 1) * LANES] for i in range(width // LANES)]
    return strips[0::2], strips[1::2]


def per_device(
    reps,
    size,
    tokens,
    segment_ids,
    w_qkv,
    w_out,
    w_up,
    w_down,
    norm_gains,
    norm_shifts,
    proj_biases,
    up_bias,
    cotangent,
):
    count = tokens.shape[1]
    seq_len = segment_ids.shape[1]
    tile = min(512, count)
    me = lax.axis_index("grp")
    rep = lax.axis_index("rep")
    seg_row = segment_ids[0]
    first_row = me * count
    own_seg = lax.dynamic_slice_in_dim(seg_row, first_row, count, 0)
    seg_col = jnp.broadcast_to(own_seg[:, None], (count, 128))
    starts = own_seg[0::tile]
    ends = own_seg[tile - 1 :: tile]
    low = jnp.sum((seg_row[None, :] < starts[:, None]).astype(jnp.int32), axis=1) // count
    high = (jnp.sum((seg_row[None, :] <= ends[:, None]).astype(jnp.int32), axis=1) - 1) // count + 1
    info = jnp.concatenate([me[None].astype(jnp.int32), low, high])
    seg_row = seg_row[None]

    mixed_qkv = jnp.concatenate([w_qkv[:, :D], key_value_mixed(w_qkv[:, D:])], axis=1)
    near_qkv = far_rows(mixed_qkv, rep, size, reps, True, (), (), ())
    first_far, last_far = near_qkv[1][2], near_qkv[-1][2]
    starts_qkv, pieces_qkv = both_cores(near_qkv, swap(mixed_qkv, "grp", size, 1), size, me, w_qkv.shape[0])
    other_out, other_up, other_down = [swap(weight, "grp", size, 1) for weight in (w_out, w_up, w_down)]
    qkv_full = place_rows(w_qkv, size, starts_qkv, pieces_qkv)

    source = tokens[0].astype(F32)
    normed = layer_norm(source, norm_gains[0], norm_shifts[0]).astype(BF16)
    normed_all = after(normed, first_far)[None]
    far_tokens = None
    for bit in list(range(1, bits_of(size))) + [0]:
        got = swap(normed_all, "grp", size, 1 << bit)
        if bit:
            far_tokens = got = after(got, last_far)
        normed_all = jnp.concatenate([normed_all, got], axis=0)
    normed_all = normed_all.reshape(seq_len, D)
    value_bias = proj_biases[1].reshape(PAIRS, LANES)
    bias = jnp.stack([jnp.zeros_like(value_bias), value_bias], axis=1).reshape(-1)
    shift = jnp.concatenate([proj_biases[0], bias])
    qkv_all = (add_rows(normed_all, qkv_full) + shift).astype(BF16)
    heads = (info, after(qkv_all, other_out, other_up, other_down))
    shapes = (seg_col, seg_row, count, seq_len, size, tile)
    part = PAIRS // 2
    earlier = attend(0, part, *heads, (), *shapes)
    near_up = far_rows(w_up, rep, size, reps, True, (far_tokens,), earlier, ())
    near_out = far_rows(w_out, rep, size, reps, False, (far_tokens,), earlier, ())
    earlier = [after(value, near_up[1][2], near_out[1][2]) for value in earlier]
    attended_f, attended, lse, lse_row = attend(part, part, *heads, earlier, *shapes)
    near_up = [(near, first, after(piece, attended)) for near, first, piece in near_up]
    near_down = far_rows(w_down, rep, size, reps, True, (near_up[1][2],), (attended,), ())
    starts_out, pieces_out = both_cores(near_out, other_out, size, me, w_out.shape[0], (attended,))
    starts_up, pieces_up = both_cores(near_up, other_up, size, me, w_up.shape[0])
    out_full = place_rows(w_out, size, starts_out, pieces_out)
    middle = source + add_rows(attended, out_full) + proj_biases[2]
    up_full = place_rows(w_up, size, starts_up, pieces_up)
    second = layer_norm(middle, norm_gains[1], norm_shifts[1]).astype(BF16)
    hidden_pre = add_rows(second, up_full) + up_bias
    hidden = jax.nn.gelu(hidden_pre).astype(BF16)
    upstream = cotangent[0]
    upstream_f = upstream.astype(F32)
    hidden_theirs, hidden_mine = by_core(hidden, me, size)
    down_theirs = other_grad(hidden_theirs, upstream)
    near_down = [(near, first, after(piece, hidden)) for near, first, piece in near_down]
    starts_down, pieces_down = both_cores(near_down, other_down, size, me, w_down.shape[0], (down_theirs,))
    down_full = place_rows(w_down, size, starts_down, pieces_down)
    hidden_grad = back_rows(after(upstream, down_theirs), down_full)
    _, gelu_pull = jax.vjp(jax.nn.gelu, hidden_pre)
    pre_grad = gelu_pull(hidden_grad)[0].astype(BF16)
    second_theirs, second_mine = by_core(second, me, size)
    up_theirs = other_grad(second_theirs, pre_grad)
    down_part = core_grad(down_theirs, after(hidden_mine, up_theirs), upstream, size, pre_grad)
    down_send, down_keep = group_step(down_part, bits_of(size) - 1, me)

    up_part = core_grad(up_theirs, second_mine, after(pre_grad, down_send), size, down_send)
    up_send, up_keep = rep_halves(up_part, rep)

    second_grad = back_rows(after(pre_grad, up_send), up_full)
    _, second_pull = jax.vjp(layer_norm, middle, norm_gains[1], norm_shifts[1])
    middle_part, gain_second, shift_second = second_pull(second_grad)
    middle_grad = upstream_f + middle_part
    branch_grad = middle_grad.astype(BF16)
    dout = back_rows(branch_grad, out_full).astype(BF16)
    row = lax.broadcasted_iota(jnp.int32, (8 * PAIRS, D), 0)
    minor = row % 8 - 2
    lane_head = lax.broadcasted_iota(jnp.int32, (8 * PAIRS, D), 1) // HD
    picks = ((row // 8 * 2 + minor == lane_head) & (minor >= 0) & (minor < 2)).astype(F32)
    delta_row = jnp.einsum(
        "ed,td->et", picks, dout.astype(F32) * attended_f, precision=lax.Precision.HIGHEST
    ).reshape(PAIRS, 8, count)

    attended_theirs, attended_mine = by_core(attended, me, size)
    normed_theirs, normed_mine = by_core(normed, me, size)
    out_theirs = other_grad(attended_theirs, after(branch_grad, dout))
    queries_one = query_grads(0, part, *heads, after(dout, up_send, out_theirs, delta_row), attended_f, lse, *shapes)

    out_part = core_grad(out_theirs, attended_mine, after(branch_grad, queries_one), size, queries_one)
    down_part = add_low(down_keep, swap(down_send, "grp", size, size // 2, queries_one))
    down_send, down_keep = rep_halves(group_sum(down_part, me, size)[0], rep)
    up_part = add_low(up_keep, swap(up_send, "rep", reps, 1, queries_one))
    up_send, up_keep = group_step(up_part, bits_of(size) - 1, me)
    queries_two = query_grads(part, part, *heads, after(dout, up_send, down_send, out_part), attended_f, lse, *shapes)
    down_part = add_low(down_keep, swap(down_send, "rep", reps, 1, queries_two))
    up_part = add_low(up_keep, swap(up_send, "grp", size, size // 2, queries_two))
    up_part = group_sum(up_part, me, size)[0]
    both_part = jnp.concatenate([down_part, as_rows(up_part)], axis=0)
    stats = gather_later(lse_row + delta_row, size, queries_one, queries_two)
    dout_all = gather_later(dout, size, queries_one, queries_two).reshape(seq_len, D)

    both_queries = jnp.concatenate([queries_one, queries_two], axis=1)
    query_theirs = other_grad(normed_theirs, both_queries)
    mixed_one = key_grads(0, part, *heads, after(dout_all, query_theirs, both_part, stats), stats, *shapes)

    query_part = core_grad(query_theirs, normed_mine, after(both_queries, mixed_one), size, mixed_one)
    pair_part = jnp.concatenate([query_part, out_part], axis=1)
    pair_send, pair_keep = group_step(pair_part, bits_of(size) - 1, me)
    one_theirs = other_grad(normed_theirs, mixed_one)
    both_part = scatter_far(both_part, rep, reps, mixed_one)
    mixed_two = key_grads(
        part, part, *heads, after(dout_all, one_theirs, pair_send, both_part), stats, *shapes
    )

    two_theirs = other_grad(normed_theirs, mixed_two)
    joined_grad = jnp.concatenate([both_queries, mixed_one, mixed_two], axis=1)
    normed_grad = back_rows(after(joined_grad, two_theirs), qkv_full)
    _, first_pull = jax.vjp(layer_norm, source, norm_gains[0], norm_shifts[0])
    source_part, gain_first, shift_first = first_pull(normed_grad)
    input_grad = middle_grad + source_part
    one_part = core_grad(one_theirs, normed_mine, after(mixed_one, mixed_two), size, mixed_two)
    pair_part = add_low(pair_keep, swap(pair_send, "grp", size, size // 2, mixed_two))
    pair_part = group_sum(pair_part, me, size)[0]
    one_part = group_sum(one_part, me, size, gain_first)[0]
    both_every = share_far(both_part, rep, reps, mixed_two)
    pair_send, pair_keep = rep_halves(pair_part, rep)
    pair_part = add_low(pair_keep, swap(pair_send, "rep", reps, 1, gain_first))

    two_part = core_grad(two_theirs, normed_mine, after(mixed_two, gain_first), size, gain_first)
    block_out = middle + add_rows(after(hidden, two_part), down_full) + proj_biases[3]
    block_out = block_out.astype(BF16)
    two_part = group_sum(two_part, me, size, block_out)[0]
    pace = [two_part]
    mixed_send, mixed_keep = rep_halves(jnp.concatenate([one_part, two_part], axis=0), rep)
    mixed_part = add_low(mixed_keep, swap(mixed_send, "rep", reps, 1))
    pace.append(mixed_part)
    pair_part = scatter_far(after(pair_part, block_out), rep, reps, mixed_part)
    both_got = swap(both_every, "rep", reps, 1, mixed_part)
    mixed_part = scatter_far(mixed_part, rep, reps)
    pace.append(mixed_part)
    pair_every = share_far(pair_part, rep, reps, mixed_part)
    mixed_every = share_far(mixed_part, rep, reps)
    pace.append(mixed_every)
    pair_got = swap(pair_every, "rep", reps, 1, mixed_every)
    mixed_got = swap(mixed_every, "rep", reps, 1)

    rows = w_qkv.shape[0]
    tall = w_down.shape[0] // 2
    grad_down = in_order(both_every[:tall], both_got[:tall], rep)
    wide = [
        in_order(both_every[i : i + rows // 2], both_got[i : i + rows // 2], rep)
        for i in range(tall, both_every.shape[0], rows // 2)
    ]
    grad_up = jnp.concatenate(wide, axis=1)
    pair_grad = in_order(pair_every, pair_got, rep).astype(F32)
    mixed_grad = in_order(mixed_every, mixed_got, rep).astype(F32)
    one_keys, one_values = key_value_apart(mixed_grad[:rows])
    two_keys, two_values = key_value_apart(mixed_grad[rows:])
    grad_qkv = jnp.concatenate([pair_grad[:rows]] + one_keys + two_keys + one_values + two_values, axis=1)
    grad_out = pair_grad[rows:]

    joined_sum = jnp.sum(joined_grad.astype(F32), axis=0, keepdims=True)
    value_sum = joined_sum[:, D:].reshape(PAIRS, 2, LANES)[:, 1].reshape(1, D)
    vectors = jnp.concatenate(
        [
            gain_first[None],
            gain_second[None],
            shift_first[None],
            shift_second[None],
            joined_sum[:, :D],
            value_sum,
            jnp.sum(branch_grad.astype(F32), axis=0, keepdims=True),
            jnp.sum(upstream_f, axis=0, keepdims=True),
            jnp.sum(pre_grad.astype(F32), axis=0).reshape(FF // D, D),
        ],
        axis=0,
    )
    vectors = total_vector(vectors, size, reps, pace)
    return (
        block_out[None],
        input_grad[None],
        grad_qkv,
        grad_out,
        grad_up.astype(F32),
        grad_down.astype(F32),
        vectors[:2],
        vectors[2:4],
        vectors[4:8],
        vectors[8:].reshape(-1),
    )


def solution(mesh):
    return jax.shard_map(
        functools.partial(per_device, mesh.shape["rep"], mesh.shape["grp"]),
        mesh=mesh,
        in_specs=(
            P("rep", "grp", None),
            P("rep", None),
            P("grp", None),
            P("grp", None),
            P("grp", None),
            P("grp", None),
            P(),
            P(),
            P(),
            P(),
            P("rep", "grp", None),
        ),
        out_specs=(
            P("rep", "grp", None),
            P("rep", "grp", None),
            P("grp", None),
            P("grp", None),
            P("grp", None),
            P("grp", None),
            P(),
            P(),
            P(),
            P(),
        ),
        check_vma=False,
    )
```

```python
import functools
import math

import jax
import jax.numpy as jnp
from jax import lax
from jax.experimental import pallas as pl
from jax.experimental.pallas import tpu as pltpu
from jax.sharding import PartitionSpec as P

D = 768
H = 12
HD = 64
FF = 3072
PAIRS = H // 2
LANES = 2 * HD
NEG = -1e30
SCALE = 1.0 / math.sqrt(HD)
F32 = jnp.float32
BF16 = jnp.bfloat16


def layer_norm(values, gain_row, shift_row):
    centre = values - jnp.mean(values, axis=-1, keepdims=True)
    spread = jnp.mean(centre * centre, axis=-1, keepdims=True)
    return centre * lax.rsqrt(spread + 1e-05) * gain_row + shift_row


def add_rows(left, piece):
    return jnp.dot(left, piece, preferred_element_type=F32)


def back_rows(right, piece):
    return jnp.einsum("te,ce->tc", right, piece, preferred_element_type=F32)


def token_product(left, right):
    return jnp.einsum("tc,te->ce", left, right, preferred_element_type=F32)


def after(value, *others):
    return lax.optimization_barrier((value,) + others)[0]


def swap(value, axis, size, mask, *until):
    got = lax.ppermute(value, axis, [(i, i ^ mask) for i in range(size)])
    return after(got, *until) if until else got


def bits_of(size):
    return size.bit_length() - 1


def gather_pieces(value, size, later, until_far, until_core):
    pieces = [value]
    for bit in range(1, bits_of(size)):
        mask = 1 << bit
        pairs = [(i, i ^ mask) for i in range(size) if i & mask or not later]
        pieces += [after(lax.ppermute(piece, "grp", pairs), *until_far) for piece in pieces]
    sent = [after(value, *until_far)] + pieces[1:] if later else pieces
    return pieces + [swap(piece, "grp", size, 1, *until_core) for piece in sent]


def block_place(block, me, size):
    near = block ^ me
    return (near >> 1) | ((near & 1) << (bits_of(size) - 1))


def far_rows(weight, rep, size, reps, spread, before, y_until, x_until):
    rows = weight.shape[0]
    side = rep & 1
    half = rows // 2
    spread = spread and half % 16 == 0
    pieces = [(0, 0, weight)]
    for bit in range(1, bits_of(size)):
        mask = 1 << bit
        found = []
        for near, first, piece in pieces:
            if spread and near == 0:
                part = lax.dynamic_slice_in_dim(piece, side * half, half, 0)
                got = swap(after(part, *before), "grp", size, mask, *y_until)
                found.append((near | mask, side * half, got))
                found.append((near | mask, (1 - side) * half, swap(got, "rep", reps, 1, *x_until)))
            else:
                found.append((near | mask, first, swap(after(piece, *before), "grp", size, mask, *y_until)))
        pieces = pieces + found
    return pieces


def both_cores(pieces, own_other, size, me, rows, until=()):
    starts, found = [], []
    for near, first, piece in pieces:
        starts += [(me ^ near) * rows + first, (me ^ near ^ 1) * rows + first]
        other = own_other if near == 0 else swap(piece, "grp", size, 1, *until)
        found += [piece, other]
    return starts, found


def place_kernel(counts, columns, starts, *refs):
    pieces, (out, sem) = refs[:-2], refs[-2:]
    copies = []
    for i, count in enumerate(counts):
        start = pl.multiple_of(starts[i] * 16, 16)
        for source, target, width in columns:
            copies.append(
                pltpu.make_async_copy(
                    pieces[i].at[:, pl.ds(source, width)],
                    out.at[pl.ds(start, count), pl.ds(target, width)],
                    sem.at[len(copies)],
                )
            )
    for copy in copies:
        copy.start()
    for copy in copies:
        copy.wait()


def place_rows(weight, size, starts, pieces, columns=None):
    rows, width = weight.shape
    counts = [piece.shape[0] for piece in pieces]
    columns = columns or [(0, 0, width)]
    anywhere = pl.BlockSpec(memory_space=pl.ANY)
    return pl.pallas_call(
        functools.partial(place_kernel, counts, columns),
        grid_spec=pltpu.PrefetchScalarGridSpec(
            num_scalar_prefetch=1,
            grid=(1,),
            in_specs=[anywhere] * len(pieces),
            out_specs=pl.BlockSpec((size * rows, width), lambda i, starts: (0, 0)),
            scratch_shapes=[pltpu.SemaphoreType.DMA((len(pieces) * len(columns),))],
        ),
        out_shape=jax.ShapeDtypeStruct((size * rows, width), weight.dtype),
        compiler_params=pltpu.CompilerParams(vmem_limit_bytes=40 * 1024 * 1024),
        cost_estimate=pl.CostEstimate(
            flops=0, bytes_accessed=4 * size * rows * width, transcendentals=0
        ),
    )(jnp.stack(starts).astype(jnp.int32) // 16, *pieces)


def key_value_mixed():
    moves = [(0, 0, D)]
    for pair in range(PAIRS):
        target = D + 2 * LANES * pair
        moves += [(D + LANES * pair, target, LANES), (2 * D + LANES * pair, target + LANES, LANES)]
    return moves


def by_core(left, me, size):
    rows = left.shape[1] // size
    core = me & 1
    if rows % 128 == 0:
        return [
            jnp.concatenate(
                [lax.dynamic_slice_in_dim(left, (2 * i + which) * rows, rows, 1) for i in range(size // 2)], axis=1
            )
            for which in (1 - core, core)
        ]
    strips = [left[:, i * rows : (i + 1) * rows] for i in range(size)]
    even = jnp.concatenate(strips[0::2], axis=1)
    odd = jnp.concatenate(strips[1::2], axis=1)
    return jnp.where(core == 0, odd, even), jnp.where(core == 0, even, odd)


def group_step(part, bit, me):
    size_left, rows, columns = part.shape
    split = part.reshape(2, size_left // 2, rows, columns)
    side = (me >> bit) & 1
    send = lax.dynamic_index_in_dim(split, 1 - side, 0, keepdims=False)
    keep = lax.dynamic_index_in_dim(split, side, 0, keepdims=False)
    return send, keep


def group_sum(part, me, size, *until):
    for bit in range(bits_of(part.shape[0]), 0, -1):
        send, keep = group_step(part, bit, me)
        part = add_low(keep, swap(send, "grp", size, 1 << bit, *until))
    return part


def add_low(keep, got):
    return (keep.astype(F32) + got.astype(F32)).astype(BF16)


def rep_halves(part, rep):
    axis = part.ndim - 2
    half = part.shape[axis] // 2
    side = rep & 1
    send = lax.dynamic_slice_in_dim(part, (1 - side) * half, half, axis)
    keep = lax.dynamic_slice_in_dim(part, side * half, half, axis)
    return send, keep


def scatter_far(part, rep, reps, *until):
    count = reps // 2
    place = rep >> 1
    pieces = part.reshape(count, -1, part.shape[1])
    total = lax.dynamic_index_in_dim(pieces, place, 0, keepdims=False).astype(F32)
    for mask in range(1, count):
        send = lax.dynamic_index_in_dim(pieces, place ^ mask, 0, keepdims=False)
        total = total + swap(send, "rep", reps, mask << 1, *until).astype(F32)
    return total.astype(BF16)


def share_far(own, rep, reps, *until):
    count = reps // 2
    place = rep >> 1
    near = [own] + [swap(own, "rep", reps, mask << 1, *until) for mask in range(1, count)]
    ordered = []
    for i in range(count):
        value = near[i]
        for j in range(1, count):
            value = jnp.where(place == j, near[i ^ j], value)
        ordered.append(value)
    return jnp.concatenate(ordered, axis=0)


def as_rows(part):
    return jnp.concatenate([part[:, i : i + D] for i in range(0, part.shape[1], D)], axis=0)


def in_order(own, got, rep):
    side = rep & 1
    low, high = jnp.where(side == 0, own, got), jnp.where(side == 0, got, own)
    return jnp.concatenate([low, high], axis=0)


def total_vector(value, size, reps, pace):
    steps = [("grp", 0), ("rep", 0)] + [("grp", bit) for bit in range(1, bits_of(size))]
    steps += [("rep", bit) for bit in range(1, bits_of(reps))]
    for i, (axis, bit) in enumerate(steps):
        count = size if axis == "grp" else reps
        value = value + swap(value, axis, count, 1 << bit, pace[min(i, len(pace) - 1)])
    return value


def other_grad(left, right):
    return token_product(left, right).astype(BF16)


def core_grad(theirs, left, right, size):
    got = swap(theirs, "grp", size, 1).astype(F32)
    part = (token_product(left, right) + got).astype(BF16)
    return part.reshape(size // 2, -1, part.shape[1])


def dot_nt(left, right):
    return lax.dot_general(left, right, (((1,), (1,)), ((), ())), preferred_element_type=F32)


def dot_nn(left, right):
    return lax.dot_general(left, right, (((1,), (0,)), ((), ())), preferred_element_type=F32)


def one_head(pair, head):
    lane = lax.broadcasted_iota(jnp.int32, pair.shape, 1)
    inside = (lane < HD) if head == 0 else (lane >= HD)
    return jnp.where(inside, pair, jnp.zeros_like(pair))


def per_head(first, second, shape):
    lane = lax.broadcasted_iota(jnp.int32, shape, 1)
    return jnp.where(lane < HD, first, second)


def start_of(block, me, size, count):
    return pl.multiple_of(block_place(block, me, size) * count, count)


def query_mask(info, qseg, kseg, bias, tile, count):
    me = info[0]
    for q in range(count // tile):
        rows = pl.ds(q * tile, tile)

        def fill(block, _):
            columns = pl.ds(pl.multiple_of(block * count, count), count)
            q_pos = me * count + q * tile + lax.broadcasted_iota(jnp.int32, (tile, count), 0)
            k_pos = block * count + lax.broadcasted_iota(jnp.int32, (tile, count), 1)
            seen = (k_pos <= q_pos) & (qseg[rows, 0:1] == kseg[0:1, columns])
            bias[rows, columns] = jnp.where(seen, 0.0, NEG)
            return 0

        lax.fori_loop(info[1 + q], me + 1, fill, 0)


def attend_kernel(size, tile, skip, info, q_ref, k_ref, v_ref, qseg, kseg, *refs):
    out, out_low, lse, lse_row, bias = refs[skip:]
    count = q_ref.shape[0]
    me = info[0]

    @pl.when(pl.program_id(0) == 0)
    def _():
        query_mask(info, qseg, kseg, bias, tile, count)

    for q in range(count // tile):
        rows = pl.ds(q * tile, tile)
        queries = q_ref[rows, :] * jnp.asarray(SCALE, BF16)

        def step(block, carry):
            tops, sums, total = carry
            start = start_of(block, me, size, count)
            keys = k_ref[pl.ds(start, count), :]
            values = v_ref[pl.ds(start, count), :]
            add = bias[rows, pl.ds(pl.multiple_of(block * count, count), count)]
            new_tops, new_sums, shrinks = [], [], []
            gain = jnp.zeros((tile, LANES), F32)
            for head in range(2):
                scores = dot_nt(queries, one_head(keys, head)) + add
                top = jnp.maximum(tops[head], jnp.max(scores, axis=1, keepdims=True))
                weights = jnp.exp(scores - top)
                shrink = jnp.exp(tops[head] - top)
                new_tops.append(top)
                shrinks.append(shrink)
                new_sums.append(sums[head] * shrink + jnp.sum(weights, axis=1, keepdims=True))
                gain = gain + dot_nn(weights.astype(BF16), one_head(values, head))
            total = total * per_head(shrinks[0], shrinks[1], total.shape) + gain
            return (tuple(new_tops), tuple(new_sums), total)

        column = jnp.zeros((tile, 1), F32)
        tops, sums, total = lax.fori_loop(
            info[1 + q],
            me + 1,
            step,
            ((column + NEG, column + NEG), (column, column), jnp.zeros((tile, LANES), F32)),
        )
        shape = (tile, LANES)
        result = total / per_head(sums[0], sums[1], shape)
        log_total = per_head(tops[0] + jnp.log(sums[0]), tops[1] + jnp.log(sums[1]), shape)
        out[rows, :] = result
        out_low[rows, :] = result.astype(BF16)
        lse[rows, :] = log_total
        turned = log_total.T
        lse_row[0, :, rows] = jnp.zeros((8, tile), F32)
        lse_row[0, 0:1, rows] = turned[0:1, :]
        lse_row[0, 1:2, rows] = turned[HD : HD + 1, :]


def query_grad_kernel(size, tile, info, q_ref, k_ref, v_ref, dout, out, lse, qseg, kseg, dq, bias):
    count = q_ref.shape[0]
    me = info[0]

    @pl.when(pl.program_id(0) == 0)
    def _():
        query_mask(info, qseg, kseg, bias, tile, count)

    for q in range(count // tile):
        rows = pl.ds(q * tile, tile)
        queries = q_ref[rows, :] * jnp.asarray(SCALE, BF16)
        douts = dout[rows, :]
        both = douts.astype(F32) * out[rows, :]
        deltas = [jnp.sum(one_head(both, head), axis=1, keepdims=True) for head in range(2)]
        logs = [lse[rows, 0:1], lse[rows, HD : HD + 1]]

        def step(block, total):
            start = start_of(block, me, size, count)
            keys = k_ref[pl.ds(start, count), :]
            values = v_ref[pl.ds(start, count), :]
            add = bias[rows, pl.ds(pl.multiple_of(block * count, count), count)]
            for head in range(2):
                one_keys = one_head(keys, head)
                scores = dot_nt(queries, one_keys) + add
                probs = jnp.exp(scores - logs[head])
                prob_grad = dot_nt(douts, one_head(values, head))
                score_grad = (probs * (prob_grad - deltas[head])).astype(BF16)
                total = total + dot_nn(score_grad, one_keys)
            return total

        total = lax.fori_loop(info[1 + q], me + 1, step, jnp.zeros((tile, LANES), F32))
        dq[rows, :] = (total * SCALE).astype(BF16)


def key_grad_kernel(size, tile, info, k_ref, v_ref, q_ref, kseg, qseg, *refs):
    pieces, stat_pieces = refs[:size], refs[size : 2 * size]
    dkv, bias, dout, stats = refs[-4:]
    count = k_ref.shape[0]
    me = info[0]
    for i in range(size):
        dout[pl.ds(i * count, count), :] = pieces[i][...]
        stats[i] = stat_pieces[i][0]
    first = 1 + count // tile

    @pl.when(pl.program_id(0) == 0)
    def _():
        for k in range(count // tile):
            rows = pl.ds(k * tile, tile)

            def fill(block, _):
                columns = pl.ds(pl.multiple_of(block * count, count), count)
                k_pos = me * count + k * tile + lax.broadcasted_iota(jnp.int32, (tile, count), 0)
                q_pos = block * count + lax.broadcasted_iota(jnp.int32, (tile, count), 1)
                seen = (k_pos <= q_pos) & (kseg[rows, 0:1] == qseg[0:1, columns])
                bias[rows, columns] = jnp.where(seen, 0.0, NEG)
                return 0

            lax.fori_loop(me, info[first + k], fill, 0)

    for k in range(count // tile):
        rows = pl.ds(k * tile, tile)
        keys = k_ref[rows, :]
        values = v_ref[rows, :]

        def step(block, carry):
            key_total, value_total = carry
            place = block_place(block, me, size)
            start = pl.multiple_of(place * count, count)
            queries = q_ref[pl.ds(start, count), :] * jnp.asarray(SCALE, BF16)
            douts = dout[pl.ds(start, count), :]
            add = bias[rows, pl.ds(pl.multiple_of(block * count, count), count)]
            for head in range(2):
                one_queries = one_head(queries, head)
                one_douts = one_head(douts, head)
                scores = dot_nt(keys, one_queries) + add
                probs = jnp.exp(scores - stats[place, head : head + 1, :])
                prob_grad = dot_nt(values, one_douts)
                score_grad = probs * (prob_grad - stats[place, 2 + head : 3 + head, :])
                value_total = value_total + dot_nn(probs.astype(BF16), one_douts)
                key_total = key_total + dot_nn(score_grad.astype(BF16), one_queries)
            return (key_total, value_total)

        empty = jnp.zeros((tile, LANES), F32)
        key_total, value_total = lax.fori_loop(me, info[first + k], step, (empty, empty))
        dkv[rows, :LANES] = key_total.astype(BF16)
        dkv[rows, LANES:] = value_total.astype(BF16)


def strip(rows, first, stride=1):
    return pl.BlockSpec((rows, LANES), lambda p, info: (0, first + stride * p))


def whole(shape):
    return pl.BlockSpec(shape, lambda p, info: (0,) * len(shape))


def paired(count, first):
    return pl.BlockSpec((1, 8, count), lambda p, info: (first + p, 0, 0))


def call(body, in_specs, out_specs, out_shape, count, seq_len, products, pairs, mib=60, aliases=None, more_scratch=()):
    return pl.pallas_call(
        body,
        grid_spec=pltpu.PrefetchScalarGridSpec(
            num_scalar_prefetch=1,
            grid=(pairs,),
            in_specs=in_specs,
            out_specs=out_specs,
            scratch_shapes=[pltpu.VMEM((count, seq_len), F32), *more_scratch],
        ),
        out_shape=out_shape,
        input_output_aliases=aliases or {},
        compiler_params=pltpu.CompilerParams(vmem_limit_bytes=mib * 1024 * 1024),
        cost_estimate=pl.CostEstimate(
            flops=products * 2 * count * count * 2 * 256 * 2 * pairs,
            bytes_accessed=8 * 1024 * 1024,
            transcendentals=count * count * 4 * pairs,
        ),
    )


def key_value_strips(rows, first):
    return [strip(rows, PAIRS + 2 * first, 2), strip(rows, PAIRS + 2 * first + 1, 2)]


def attend(first, pairs, info, qkv_all, earlier, ready, seg_col, seg_row, count, seq_len, size, tile):
    out = jax.ShapeDtypeStruct((count, D), F32)
    return call(
        functools.partial(attend_kernel, size, tile, len(earlier) + len(ready)),
        [strip(count, first)]
        + key_value_strips(seq_len, first)
        + [whole((count, 128)), whole((1, seq_len))]
        + [pl.BlockSpec(memory_space=pl.ANY)] * (len(earlier) + len(ready)),
        [strip(count, first), strip(count, first), strip(count, first), paired(count, first)],
        [out, jax.ShapeDtypeStruct((count, D), BF16), out, jax.ShapeDtypeStruct((PAIRS, 8, count), F32)],
        count,
        seq_len,
        2,
        pairs,
        40,
        {6 + i: i for i in range(len(earlier))},
    )(info, qkv_all, qkv_all, qkv_all, seg_col, seg_row, *earlier, *ready)


def query_grads(first, pairs, info, qkv_all, dout, out, lse, seg_col, seg_row, count, seq_len, size, tile):
    return call(
        functools.partial(query_grad_kernel, size, tile),
        [strip(count, first)] + key_value_strips(seq_len, first)
        + [strip(count, first)] * 3
        + [whole((count, 128)), whole((1, seq_len))],
        strip(count, 0),
        jax.ShapeDtypeStruct((count, pairs * LANES), BF16),
        count,
        seq_len,
        3,
        pairs,
    )(info, qkv_all, qkv_all, qkv_all, dout, out, lse, seg_col, seg_row)


def key_grads(first, pairs, info, qkv_all, dout_all, stats, seg_col, seg_row, count, seq_len, size, tile):
    return call(
        functools.partial(key_grad_kernel, size, tile),
        key_value_strips(count, first)
        + [strip(seq_len, first)]
        + [whole((count, 128)), whole((1, seq_len))]
        + [strip(count, first)] * size
        + [paired(count, first)] * size,
        pl.BlockSpec((count, 2 * LANES), lambda p, info: (0, p)),
        jax.ShapeDtypeStruct((count, pairs * 2 * LANES), BF16),
        count,
        seq_len,
        4,
        pairs,
        more_scratch=[pltpu.VMEM((seq_len, LANES), BF16), pltpu.VMEM((size, 8, count), F32)],
    )(info, qkv_all, qkv_all, qkv_all, seg_col, seg_row, *dout_all, *stats)


def key_value_apart(columns):
    rows, width = columns.shape
    strips = [columns[:, i * LANES : (i + 1) * LANES] for i in range(width // LANES)]
    return strips[0::2], strips[1::2]


def per_device(
    reps,
    size,
    tokens,
    segment_ids,
    w_qkv,
    w_out,
    w_up,
    w_down,
    norm_gains,
    norm_shifts,
    proj_biases,
    up_bias,
    cotangent,
):
    count = tokens.shape[1]
    seq_len = segment_ids.shape[1]
    tile = min(512, count)
    me = lax.axis_index("grp")
    rep = lax.axis_index("rep")
    seg_row = segment_ids[0]
    first_row = me * count
    own_seg = lax.dynamic_slice_in_dim(seg_row, first_row, count, 0)
    seg_col = jnp.broadcast_to(own_seg[:, None], (count, 128))
    starts = own_seg[0::tile]
    ends = own_seg[tile - 1 :: tile]
    low = jnp.sum((seg_row[None, :] < starts[:, None]).astype(jnp.int32), axis=1) // count
    high = (jnp.sum((seg_row[None, :] <= ends[:, None]).astype(jnp.int32), axis=1) - 1) // count + 1
    info = jnp.concatenate([me[None].astype(jnp.int32), low, high])
    seg_row = seg_row[None]

    near_qkv = far_rows(w_qkv, rep, size, reps, True, (), (), ())
    first_far, last_far = near_qkv[1][2], near_qkv[-1][2]
    starts_qkv, pieces_qkv = both_cores(near_qkv, swap(w_qkv, "grp", size, 1), size, me, w_qkv.shape[0])
    other_out, other_up, other_down = [swap(weight, "grp", size, 1) for weight in (w_out, w_up, w_down)]
    qkv_full = place_rows(w_qkv, size, starts_qkv, pieces_qkv, key_value_mixed())

    source = tokens[0].astype(F32)
    normed = layer_norm(source, norm_gains[0], norm_shifts[0]).astype(BF16)
    normed_pieces = gather_pieces(after(normed, first_far), size, False, (last_far,), ())
    far_tokens = normed_pieces[1]
    normed_all = lax.optimization_barrier(jnp.concatenate(normed_pieces, axis=0))
    value_bias = proj_biases[1].reshape(PAIRS, LANES)
    bias = jnp.stack([jnp.zeros_like(value_bias), value_bias], axis=1).reshape(-1)
    shift = jnp.concatenate([proj_biases[0], bias])
    qkv_all = (add_rows(normed_all, qkv_full) + shift).astype(BF16)
    heads = (info, qkv_all)
    shapes = (seg_col, seg_row, count, seq_len, size, tile)
    part = PAIRS // 2
    earlier = attend(0, part, *heads, (), (other_out, other_up, other_down), *shapes)
    near_up = far_rows(w_up, rep, size, reps, True, (far_tokens,), earlier, ())
    near_out = far_rows(w_out, rep, size, reps, False, (far_tokens,), earlier, ())
    starts_out, pieces_out = both_cores(near_out, other_out, size, me, w_out.shape[0])
    starts_up, pieces_up = both_cores(near_up, other_up, size, me, w_up.shape[0])
    ready = pieces_out[2:] + pieces_up[2:4]
    attended_f, attended, lse, lse_row = attend(part, part, *heads, earlier, ready, *shapes)
    pieces_out[0], pieces_up[0] = after(pieces_out[0], attended), after(pieces_up[0], attended)
    near_down = far_rows(w_down, rep, size, reps, True, (near_up[1][2],), (attended,), ())
    out_full = place_rows(w_out, size, starts_out, pieces_out)
    middle = source + add_rows(attended, out_full) + proj_biases[2]
    up_full = place_rows(w_up, size, starts_up, pieces_up)
    second = layer_norm(middle, norm_gains[1], norm_shifts[1]).astype(BF16)
    hidden_pre = add_rows(second, up_full) + up_bias
    hidden = jax.nn.gelu(hidden_pre).astype(BF16)
    upstream = cotangent[0]
    upstream_f = upstream.astype(F32)
    hidden_theirs, hidden_mine = by_core(hidden, me, size)
    down_theirs = other_grad(hidden_theirs, upstream)
    near_down = [(near, first, after(piece, hidden)) for near, first, piece in near_down]
    starts_down, pieces_down = both_cores(near_down, other_down, size, me, w_down.shape[0], (down_theirs,))
    down_full = place_rows(w_down, size, starts_down, pieces_down)
    hidden_grad = back_rows(after(upstream, down_theirs), down_full)
    _, gelu_pull = jax.vjp(jax.nn.gelu, hidden_pre)
    pre_grad = gelu_pull(hidden_grad)[0].astype(BF16)
    second_theirs, second_mine = by_core(second, me, size)
    up_theirs = other_grad(second_theirs, pre_grad)
    down_part = core_grad(down_theirs, after(hidden_mine, up_theirs), upstream, size)
    down_send, down_keep = group_step(down_part, bits_of(size) - 1, me)

    up_part = core_grad(up_theirs, second_mine, after(pre_grad, down_send), size)
    up_send, up_keep = rep_halves(up_part, rep)

    second_grad = back_rows(after(pre_grad, up_send), up_full)
    _, second_pull = jax.vjp(layer_norm, middle, norm_gains[1], norm_shifts[1])
    middle_part, gain_second, shift_second = second_pull(second_grad)
    middle_grad = upstream_f + middle_part
    branch_grad = middle_grad.astype(BF16)
    dout = back_rows(branch_grad, out_full).astype(BF16)
    row = lax.broadcasted_iota(jnp.int32, (8 * PAIRS, D), 0)
    minor = row % 8 - 2
    lane_head = lax.broadcasted_iota(jnp.int32, (8 * PAIRS, D), 1) // HD
    picks = ((row // 8 * 2 + minor == lane_head) & (minor >= 0) & (minor < 2)).astype(F32)
    delta_row = jnp.einsum(
        "ed,td->et", picks, dout.astype(F32) * attended_f, precision=lax.Precision.HIGHEST
    ).reshape(PAIRS, 8, count)

    attended_theirs, attended_mine = by_core(after(attended, dout), me, size)
    out_theirs = other_grad(attended_theirs, after(branch_grad, dout))
    queries_one = query_grads(0, part, *heads, after(dout, up_send, out_theirs, delta_row), attended_f, lse, *shapes)

    out_part = core_grad(out_theirs, attended_mine, after(branch_grad, queries_one), size)
    down_part = add_low(down_keep, swap(down_send, "grp", size, size // 2, queries_one))
    down_send, down_keep = rep_halves(group_sum(down_part, me, size)[0], rep)
    up_part = add_low(up_keep, swap(up_send, "rep", reps, 1, queries_one))
    up_send, up_keep = group_step(up_part, bits_of(size) - 1, me)
    queries_two = query_grads(part, part, *heads, after(dout, up_send, down_send, out_part), attended_f, lse, *shapes)
    down_part = add_low(down_keep, swap(down_send, "rep", reps, 1, queries_two))
    up_part = add_low(up_keep, swap(up_send, "grp", size, size // 2, queries_two))
    up_part = group_sum(up_part, me, size)[0]
    both_part = jnp.concatenate([down_part, as_rows(up_part)], axis=0)
    stats = gather_pieces(lse_row + delta_row, size, True, (queries_two,), ())
    dout_all = gather_pieces(dout, size, True, (queries_two,), ())

    normed_theirs, normed_mine = by_core(after(normed, queries_one), me, size)
    both_queries = jnp.concatenate([queries_one, queries_two], axis=1)
    query_theirs = other_grad(normed_theirs, after(both_queries, both_part))
    mixed_one = key_grads(0, part, *heads, [after(dout_all[0], query_theirs, both_part)] + dout_all[1:], stats, *shapes)

    query_part = core_grad(query_theirs, normed_mine, after(both_queries, mixed_one), size)
    pair_part = jnp.concatenate([query_part, out_part], axis=1)
    pair_send, pair_keep = group_step(pair_part, bits_of(size) - 1, me)
    one_theirs = other_grad(normed_theirs, mixed_one)
    both_part = scatter_far(both_part, rep, reps, mixed_one)
    mixed_two = key_grads(
        part, part, *heads, [after(dout_all[0], one_theirs, pair_send, both_part)] + dout_all[1:], stats, *shapes
    )

    two_theirs = other_grad(normed_theirs, mixed_two)
    one_part = core_grad(one_theirs, normed_mine, after(mixed_one, two_theirs), size)
    two_part = core_grad(two_theirs, normed_mine, after(mixed_two, one_part), size)
    mixed_part = jnp.concatenate([one_part, two_part], axis=1)
    mixed_send, mixed_keep = group_step(mixed_part, bits_of(size) - 1, me)
    pair_part = add_low(after(pair_keep, mixed_send), swap(pair_send, "grp", size, size // 2, mixed_two))
    pair_send, pair_keep = rep_halves(group_sum(pair_part, me, size)[0], rep)
    both_every = share_far(both_part, rep, reps, mixed_two)

    joined_grad = jnp.concatenate([both_queries, mixed_one, mixed_two], axis=1)
    normed_grad = back_rows(after(joined_grad, mixed_send, pair_send), qkv_full)
    _, first_pull = jax.vjp(layer_norm, source, norm_gains[0], norm_shifts[0])
    source_part, gain_first, shift_first = first_pull(normed_grad)
    input_grad = middle_grad + source_part
    joined_sum = jnp.sum(joined_grad.astype(F32), axis=0, keepdims=True)
    value_sum = joined_sum[:, D:].reshape(PAIRS, 2, LANES)[:, 1].reshape(1, D)
    vectors = jnp.concatenate(
        [
            gain_first[None],
            gain_second[None],
            shift_first[None],
            shift_second[None],
            joined_sum[:, :D],
            value_sum,
            jnp.sum(branch_grad.astype(F32), axis=0, keepdims=True),
            jnp.sum(upstream_f, axis=0, keepdims=True),
            jnp.sum(pre_grad.astype(F32), axis=0).reshape(FF // D, D),
        ],
        axis=0,
    )

    mixed_part = add_low(mixed_keep, swap(mixed_send, "grp", size, size // 2, vectors))
    mixed_send, mixed_keep = rep_halves(group_sum(mixed_part, me, size)[0], rep)
    pair_part = add_low(pair_keep, swap(pair_send, "rep", reps, 1, mixed_send))
    nothing = mixed_send[0:1, :].astype(F32) * 0.0
    block_out = (middle + add_rows(hidden, down_full) + (proj_biases[3] + nothing)).astype(BF16)
    pace = [mixed_send, mixed_send]
    mixed_part = add_low(mixed_keep, swap(mixed_send, "rep", reps, 1, block_out))

    both_got = swap(after(both_every, block_out), "rep", reps, 1)
    pair_part = scatter_far(pair_part, rep, reps, mixed_part)
    mixed_part = scatter_far(mixed_part, rep, reps, pair_part)
    pair_every = share_far(pair_part, rep, reps, mixed_part)
    mixed_every = share_far(mixed_part, rep, reps, pair_every)
    pace += [mixed_part, mixed_part, mixed_every]
    mixed_got = swap(mixed_every, "rep", reps, 1)
    pair_got = swap(pair_every, "rep", reps, 1, mixed_every)
    vectors = total_vector(vectors, size, reps, pace)

    rows = w_qkv.shape[0]
    tall = w_down.shape[0] // 2
    grad_down = in_order(both_every[:tall], both_got[:tall], rep)
    wide = [
        in_order(both_every[i : i + rows // 2], both_got[i : i + rows // 2], rep)
        for i in range(tall, both_every.shape[0], rows // 2)
    ]
    grad_up = jnp.concatenate(wide, axis=1)
    pair_grad = in_order(pair_every, pair_got, rep).astype(F32)
    mixed_grad = in_order(mixed_every, mixed_got, rep).astype(F32)
    one_keys, one_values = key_value_apart(mixed_grad[:rows])
    two_keys, two_values = key_value_apart(mixed_grad[rows:])
    grad_qkv = jnp.concatenate([pair_grad[:rows]] + one_keys + two_keys + one_values + two_values, axis=1)
    grad_out = pair_grad[rows:]
    return (
        block_out[None],
        input_grad[None],
        grad_qkv,
        grad_out,
        grad_up.astype(F32),
        grad_down.astype(F32),
        vectors[:2],
        vectors[2:4],
        vectors[4:8],
        vectors[8:].reshape(-1),
    )


def solution(mesh):
    return jax.shard_map(
        functools.partial(per_device, mesh.shape["rep"], mesh.shape["grp"]),
        mesh=mesh,
        in_specs=(
            P("rep", "grp", None),
            P("rep", None),
            P("grp", None),
            P("grp", None),
            P("grp", None),
            P("grp", None),
            P(),
            P(),
            P(),
            P(),
            P("rep", "grp", None),
        ),
        out_specs=(
            P("rep", "grp", None),
            P("rep", "grp", None),
            P("grp", None),
            P("grp", None),
            P("grp", None),
            P("grp", None),
            P(),
            P(),
            P(),
            P(),
        ),
        check_vma=False,
    )
```

```python
import functools
import math

import jax
import jax.numpy as jnp
from jax import lax
from jax.experimental import pallas as pl
from jax.experimental.pallas import tpu as pltpu
from jax.sharding import PartitionSpec as P

D = 768
H = 12
HD = 64
FF = 3072
PAIRS = H // 2
LANES = 2 * HD
NEG = -1e30
SCALE = 1.0 / math.sqrt(HD)
F32 = jnp.float32
BF16 = jnp.bfloat16


def layer_norm(values, gain_row, shift_row):
    centre = values - jnp.mean(values, axis=-1, keepdims=True)
    spread = jnp.mean(centre * centre, axis=-1, keepdims=True)
    return centre * lax.rsqrt(spread + 1e-05) * gain_row + shift_row


def add_rows(left, piece):
    return jnp.dot(left, piece, preferred_element_type=F32)


def back_rows(right, piece):
    return jnp.einsum("te,ce->tc", right, piece, preferred_element_type=F32)


def token_product(left, right):
    return jnp.einsum("tc,te->ce", left, right, preferred_element_type=F32)


def after(value, *others):
    return lax.optimization_barrier((value,) + others)[0]


def swap(value, axis, size, mask, *until):
    got = lax.ppermute(value, axis, [(i, i ^ mask) for i in range(size)])
    return after(got, *until) if until else got


def bits_of(size):
    return size.bit_length() - 1


def gather_pieces(value, size, later, until_far, until_core):
    pieces = [value]
    for bit in range(1, bits_of(size)):
        mask = 1 << bit
        pairs = [(i, i ^ mask) for i in range(size) if i & mask or not later]
        pieces += [after(lax.ppermute(piece, "grp", pairs), *until_far) for piece in pieces]
    sent = [after(value, *until_far)] + pieces[1:] if later else pieces
    return pieces + [swap(piece, "grp", size, 1, *until_core) for piece in sent]


def block_place(block, me, size):
    near = block ^ me
    return (near >> 1) | ((near & 1) << (bits_of(size) - 1))


def far_rows(weight, rep, size, reps, spread, before, y_until, x_until):
    rows = weight.shape[0]
    side = rep & 1
    half = rows // 2
    spread = spread and half % 16 == 0
    pieces = [(0, 0, weight)]
    for bit in range(1, bits_of(size)):
        mask = 1 << bit
        found = []
        for near, first, piece in pieces:
            if spread and near == 0:
                part = lax.dynamic_slice_in_dim(piece, side * half, half, 0)
                got = swap(after(part, *before), "grp", size, mask, *y_until)
                found.append((near | mask, side * half, got))
                found.append((near | mask, (1 - side) * half, swap(got, "rep", reps, 1, *x_until)))
            else:
                found.append((near | mask, first, swap(after(piece, *before), "grp", size, mask, *y_until)))
        pieces = pieces + found
    return pieces


def both_cores(pieces, own_other, size, me, rows, until=()):
    starts, found = [], []
    for near, first, piece in pieces:
        starts += [(me ^ near) * rows + first, (me ^ near ^ 1) * rows + first]
        other = own_other if near == 0 else swap(piece, "grp", size, 1, *until)
        found += [piece, other]
    return starts, found


def place_kernel(counts, columns, starts, *refs):
    pieces, (out, sem) = refs[:-2], refs[-2:]
    copies = []
    for i, count in enumerate(counts):
        start = pl.multiple_of(starts[i] * 16, 16)
        for source, target, width in columns:
            copies.append(
                pltpu.make_async_copy(
                    pieces[i].at[:, pl.ds(source, width)],
                    out.at[pl.ds(start, count), pl.ds(target, width)],
                    sem.at[len(copies)],
                )
            )
    for copy in copies:
        copy.start()
    for copy in copies:
        copy.wait()


def place_rows(weight, size, starts, pieces, columns=None):
    rows, width = weight.shape
    counts = [piece.shape[0] for piece in pieces]
    columns = columns or [(0, 0, width)]
    anywhere = pl.BlockSpec(memory_space=pl.ANY)
    return pl.pallas_call(
        functools.partial(place_kernel, counts, columns),
        grid_spec=pltpu.PrefetchScalarGridSpec(
            num_scalar_prefetch=1,
            grid=(1,),
            in_specs=[anywhere] * len(pieces),
            out_specs=pl.BlockSpec((size * rows, width), lambda i, starts: (0, 0)),
            scratch_shapes=[pltpu.SemaphoreType.DMA((len(pieces) * len(columns),))],
        ),
        out_shape=jax.ShapeDtypeStruct((size * rows, width), weight.dtype),
        compiler_params=pltpu.CompilerParams(vmem_limit_bytes=40 * 1024 * 1024),
        cost_estimate=pl.CostEstimate(
            flops=0, bytes_accessed=4 * size * rows * width, transcendentals=0
        ),
    )(jnp.stack(starts).astype(jnp.int32) // 16, *pieces)


def key_value_mixed():
    moves = [(0, 0, D)]
    for pair in range(PAIRS):
        target = D + 2 * LANES * pair
        moves += [(D + LANES * pair, target, LANES), (2 * D + LANES * pair, target + LANES, LANES)]
    return moves


def by_core(left, me, size):
    rows = left.shape[1] // size
    core = me & 1
    if rows % 128 == 0:
        return [
            jnp.concatenate(
                [lax.dynamic_slice_in_dim(left, (2 * i + which) * rows, rows, 1) for i in range(size // 2)], axis=1
            )
            for which in (1 - core, core)
        ]
    strips = [left[:, i * rows : (i + 1) * rows] for i in range(size)]
    even = jnp.concatenate(strips[0::2], axis=1)
    odd = jnp.concatenate(strips[1::2], axis=1)
    return jnp.where(core == 0, odd, even), jnp.where(core == 0, even, odd)


def group_step(part, bit, me):
    size_left, rows, columns = part.shape
    split = part.reshape(2, size_left // 2, rows, columns)
    side = (me >> bit) & 1
    send = lax.dynamic_index_in_dim(split, 1 - side, 0, keepdims=False)
    keep = lax.dynamic_index_in_dim(split, side, 0, keepdims=False)
    return send, keep


def group_sum(part, me, size, *until):
    for bit in range(bits_of(part.shape[0]), 0, -1):
        send, keep = group_step(part, bit, me)
        part = add_low(keep, swap(send, "grp", size, 1 << bit, *until))
    return part


def add_low(keep, got):
    return (keep.astype(F32) + got.astype(F32)).astype(BF16)


def rep_halves(part, rep):
    axis = part.ndim - 2
    half = part.shape[axis] // 2
    side = rep & 1
    send = lax.dynamic_slice_in_dim(part, (1 - side) * half, half, axis)
    keep = lax.dynamic_slice_in_dim(part, side * half, half, axis)
    return send, keep


def scatter_far(part, rep, reps, *until):
    count = reps // 2
    place = rep >> 1
    pieces = part.reshape(count, -1, part.shape[1])
    total = lax.dynamic_index_in_dim(pieces, place, 0, keepdims=False).astype(F32)
    for mask in range(1, count):
        send = lax.dynamic_index_in_dim(pieces, place ^ mask, 0, keepdims=False)
        total = total + swap(send, "rep", reps, mask << 1, *until).astype(F32)
    return total.astype(BF16)


def share_far(own, rep, reps, *until):
    count = reps // 2
    place = rep >> 1
    near = [own] + [swap(own, "rep", reps, mask << 1, *until) for mask in range(1, count)]
    ordered = []
    for i in range(count):
        value = near[i]
        for j in range(1, count):
            value = jnp.where(place == j, near[i ^ j], value)
        ordered.append(value)
    return jnp.concatenate(ordered, axis=0)


def as_rows(part):
    return jnp.concatenate([part[:, i : i + D] for i in range(0, part.shape[1], D)], axis=0)


def in_order(own, got, rep):
    side = rep & 1
    low, high = jnp.where(side == 0, own, got), jnp.where(side == 0, got, own)
    return jnp.concatenate([low, high], axis=0)


def total_vector(value, size, reps, pace, first):
    steps = [("grp", 0), ("rep", 0)] + [("grp", bit) for bit in range(1, bits_of(size))]
    steps += [("rep", bit) for bit in range(1, bits_of(reps))]
    for i, (axis, bit) in enumerate(steps):
        count = size if axis == "grp" else reps
        if (axis, bit) == ("rep", 1):
            value = value + first[0:1, :].astype(F32) * 0.0
        value = value + swap(value, axis, count, 1 << bit, pace[min(i, len(pace) - 1)])
    return value


def other_grad(left, right):
    return token_product(left, right).astype(BF16)


def core_grad(theirs, left, right, size):
    got = swap(theirs, "grp", size, 1).astype(F32)
    part = (token_product(left, right) + got).astype(BF16)
    return part.reshape(size // 2, -1, part.shape[1])


def dot_nt(left, right):
    return lax.dot_general(left, right, (((1,), (1,)), ((), ())), preferred_element_type=F32)


def dot_nn(left, right):
    return lax.dot_general(left, right, (((1,), (0,)), ((), ())), preferred_element_type=F32)


def one_head(pair, head):
    lane = lax.broadcasted_iota(jnp.int32, pair.shape, 1)
    inside = (lane < HD) if head == 0 else (lane >= HD)
    return jnp.where(inside, pair, jnp.zeros_like(pair))


def per_head(first, second, shape):
    lane = lax.broadcasted_iota(jnp.int32, shape, 1)
    return jnp.where(lane < HD, first, second)


def start_of(block, me, size, count):
    return pl.multiple_of(block_place(block, me, size) * count, count)


def query_mask(info, qseg, kseg, bias, tile, count):
    me = info[0]
    for q in range(count // tile):
        rows = pl.ds(q * tile, tile)

        def fill(block, _):
            columns = pl.ds(pl.multiple_of(block * count, count), count)
            q_pos = me * count + q * tile + lax.broadcasted_iota(jnp.int32, (tile, count), 0)
            k_pos = block * count + lax.broadcasted_iota(jnp.int32, (tile, count), 1)
            seen = (k_pos <= q_pos) & (qseg[rows, 0:1] == kseg[0:1, columns])
            bias[rows, columns] = jnp.where(seen, 0.0, NEG)
            return 0

        lax.fori_loop(info[1 + q], me + 1, fill, 0)


def attend_kernel(size, tile, skip, info, q_ref, k_ref, v_ref, qseg, kseg, *refs):
    out, out_low, lse, lse_row, bias = refs[skip:]
    count = q_ref.shape[0]
    me = info[0]

    @pl.when(pl.program_id(0) == 0)
    def _():
        query_mask(info, qseg, kseg, bias, tile, count)

    for q in range(count // tile):
        rows = pl.ds(q * tile, tile)
        queries = q_ref[rows, :] * jnp.asarray(SCALE, BF16)

        def step(block, carry):
            tops, sums, total = carry
            start = start_of(block, me, size, count)
            keys = k_ref[pl.ds(start, count), :]
            values = v_ref[pl.ds(start, count), :]
            add = bias[rows, pl.ds(pl.multiple_of(block * count, count), count)]
            new_tops, new_sums, shrinks = [], [], []
            gain = jnp.zeros((tile, LANES), F32)
            for head in range(2):
                scores = dot_nt(queries, one_head(keys, head)) + add
                top = jnp.maximum(tops[head], jnp.max(scores, axis=1, keepdims=True))
                weights = jnp.exp(scores - top)
                shrink = jnp.exp(tops[head] - top)
                new_tops.append(top)
                shrinks.append(shrink)
                new_sums.append(sums[head] * shrink + jnp.sum(weights, axis=1, keepdims=True))
                gain = gain + dot_nn(weights.astype(BF16), one_head(values, head))
            total = total * per_head(shrinks[0], shrinks[1], total.shape) + gain
            return (tuple(new_tops), tuple(new_sums), total)

        column = jnp.zeros((tile, 1), F32)
        tops, sums, total = lax.fori_loop(
            info[1 + q],
            me + 1,
            step,
            ((column + NEG, column + NEG), (column, column), jnp.zeros((tile, LANES), F32)),
        )
        shape = (tile, LANES)
        result = total / per_head(sums[0], sums[1], shape)
        log_total = per_head(tops[0] + jnp.log(sums[0]), tops[1] + jnp.log(sums[1]), shape)
        out[rows, :] = result
        out_low[rows, :] = result.astype(BF16)
        lse[rows, :] = log_total
        turned = log_total.T
        lse_row[0, :, rows] = jnp.zeros((8, tile), F32)
        lse_row[0, 0:1, rows] = turned[0:1, :]
        lse_row[0, 1:2, rows] = turned[HD : HD + 1, :]


def query_grad_kernel(size, tile, info, q_ref, k_ref, v_ref, dout, out, lse, qseg, kseg, dq, bias):
    count = q_ref.shape[0]
    me = info[0]

    @pl.when(pl.program_id(0) == 0)
    def _():
        query_mask(info, qseg, kseg, bias, tile, count)

    for q in range(count // tile):
        rows = pl.ds(q * tile, tile)
        queries = q_ref[rows, :] * jnp.asarray(SCALE, BF16)
        douts = dout[rows, :]
        both = douts.astype(F32) * out[rows, :]
        deltas = [jnp.sum(one_head(both, head), axis=1, keepdims=True) for head in range(2)]
        logs = [lse[rows, 0:1], lse[rows, HD : HD + 1]]

        def step(block, total):
            start = start_of(block, me, size, count)
            keys = k_ref[pl.ds(start, count), :]
            values = v_ref[pl.ds(start, count), :]
            add = bias[rows, pl.ds(pl.multiple_of(block * count, count), count)]
            for head in range(2):
                one_keys = one_head(keys, head)
                scores = dot_nt(queries, one_keys) + add
                probs = jnp.exp(scores - logs[head])
                prob_grad = dot_nt(douts, one_head(values, head))
                score_grad = (probs * (prob_grad - deltas[head])).astype(BF16)
                total = total + dot_nn(score_grad, one_keys)
            return total

        total = lax.fori_loop(info[1 + q], me + 1, step, jnp.zeros((tile, LANES), F32))
        dq[rows, :] = (total * SCALE).astype(BF16)


def key_grad_kernel(size, tile, info, k_ref, v_ref, q_ref, kseg, qseg, *refs):
    pieces, stat_pieces = refs[:size], refs[size : 2 * size]
    dkv, bias, dout, stats = refs[-4:]
    count = k_ref.shape[0]
    me = info[0]
    for i in range(size):
        dout[pl.ds(i * count, count), :] = pieces[i][...]
        stats[i] = stat_pieces[i][0]
    first = 1 + count // tile

    @pl.when(pl.program_id(0) == 0)
    def _():
        for k in range(count // tile):
            rows = pl.ds(k * tile, tile)

            def fill(block, _):
                columns = pl.ds(pl.multiple_of(block * count, count), count)
                k_pos = me * count + k * tile + lax.broadcasted_iota(jnp.int32, (tile, count), 0)
                q_pos = block * count + lax.broadcasted_iota(jnp.int32, (tile, count), 1)
                seen = (k_pos <= q_pos) & (kseg[rows, 0:1] == qseg[0:1, columns])
                bias[rows, columns] = jnp.where(seen, 0.0, NEG)
                return 0

            lax.fori_loop(me, info[first + k], fill, 0)

    for k in range(count // tile):
        rows = pl.ds(k * tile, tile)
        keys = k_ref[rows, :]
        values = v_ref[rows, :]

        def step(block, carry):
            key_total, value_total = carry
            place = block_place(block, me, size)
            start = pl.multiple_of(place * count, count)
            queries = q_ref[pl.ds(start, count), :] * jnp.asarray(SCALE, BF16)
            douts = dout[pl.ds(start, count), :]
            add = bias[rows, pl.ds(pl.multiple_of(block * count, count), count)]
            for head in range(2):
                one_queries = one_head(queries, head)
                one_douts = one_head(douts, head)
                scores = dot_nt(keys, one_queries) + add
                probs = jnp.exp(scores - stats[place, head : head + 1, :])
                prob_grad = dot_nt(values, one_douts)
                score_grad = probs * (prob_grad - stats[place, 2 + head : 3 + head, :])
                value_total = value_total + dot_nn(probs.astype(BF16), one_douts)
                key_total = key_total + dot_nn(score_grad.astype(BF16), one_queries)
            return (key_total, value_total)

        empty = jnp.zeros((tile, LANES), F32)
        key_total, value_total = lax.fori_loop(me, info[first + k], step, (empty, empty))
        dkv[rows, :LANES] = key_total.astype(BF16)
        dkv[rows, LANES:] = value_total.astype(BF16)


def strip(rows, first, stride=1):
    return pl.BlockSpec((rows, LANES), lambda p, info: (0, first + stride * p))


def whole(shape):
    return pl.BlockSpec(shape, lambda p, info: (0,) * len(shape))


def paired(count, first):
    return pl.BlockSpec((1, 8, count), lambda p, info: (first + p, 0, 0))


def call(body, in_specs, out_specs, out_shape, count, seq_len, products, pairs, mib=60, aliases=None, more_scratch=()):
    return pl.pallas_call(
        body,
        grid_spec=pltpu.PrefetchScalarGridSpec(
            num_scalar_prefetch=1,
            grid=(pairs,),
            in_specs=in_specs,
            out_specs=out_specs,
            scratch_shapes=[pltpu.VMEM((count, seq_len), F32), *more_scratch],
        ),
        out_shape=out_shape,
        input_output_aliases=aliases or {},
        compiler_params=pltpu.CompilerParams(vmem_limit_bytes=mib * 1024 * 1024),
        cost_estimate=pl.CostEstimate(
            flops=products * 2 * count * count * 2 * 256 * 2 * pairs,
            bytes_accessed=8 * 1024 * 1024,
            transcendentals=count * count * 4 * pairs,
        ),
    )


def key_value_strips(rows, first):
    return [strip(rows, PAIRS + 2 * first, 2), strip(rows, PAIRS + 2 * first + 1, 2)]


def attend(first, pairs, info, qkv_all, earlier, ready, seg_col, seg_row, count, seq_len, size, tile):
    out = jax.ShapeDtypeStruct((count, D), F32)
    return call(
        functools.partial(attend_kernel, size, tile, len(earlier) + len(ready)),
        [strip(count, first)]
        + key_value_strips(seq_len, first)
        + [whole((count, 128)), whole((1, seq_len))]
        + [pl.BlockSpec(memory_space=pl.ANY)] * (len(earlier) + len(ready)),
        [strip(count, first), strip(count, first), strip(count, first), paired(count, first)],
        [out, jax.ShapeDtypeStruct((count, D), BF16), out, jax.ShapeDtypeStruct((PAIRS, 8, count), F32)],
        count,
        seq_len,
        2,
        pairs,
        40,
        {6 + i: i for i in range(len(earlier))},
    )(info, qkv_all, qkv_all, qkv_all, seg_col, seg_row, *earlier, *ready)


def query_grads(first, pairs, info, qkv_all, dout, out, lse, seg_col, seg_row, count, seq_len, size, tile):
    return call(
        functools.partial(query_grad_kernel, size, tile),
        [strip(count, first)] + key_value_strips(seq_len, first)
        + [strip(count, first)] * 3
        + [whole((count, 128)), whole((1, seq_len))],
        strip(count, 0),
        jax.ShapeDtypeStruct((count, pairs * LANES), BF16),
        count,
        seq_len,
        3,
        pairs,
    )(info, qkv_all, qkv_all, qkv_all, dout, out, lse, seg_col, seg_row)


def key_grads(first, pairs, info, qkv_all, dout_all, stats, seg_col, seg_row, count, seq_len, size, tile):
    return call(
        functools.partial(key_grad_kernel, size, tile),
        key_value_strips(count, first)
        + [strip(seq_len, first)]
        + [whole((count, 128)), whole((1, seq_len))]
        + [strip(count, first)] * size
        + [paired(count, first)] * size,
        pl.BlockSpec((count, 2 * LANES), lambda p, info: (0, p)),
        jax.ShapeDtypeStruct((count, pairs * 2 * LANES), BF16),
        count,
        seq_len,
        4,
        pairs,
        more_scratch=[pltpu.VMEM((seq_len, LANES), BF16), pltpu.VMEM((size, 8, count), F32)],
    )(info, qkv_all, qkv_all, qkv_all, seg_col, seg_row, *dout_all, *stats)


def key_value_apart(columns):
    rows, width = columns.shape
    strips = [columns[:, i * LANES : (i + 1) * LANES] for i in range(width // LANES)]
    return strips[0::2], strips[1::2]


def per_device(
    reps,
    size,
    tokens,
    segment_ids,
    w_qkv,
    w_out,
    w_up,
    w_down,
    norm_gains,
    norm_shifts,
    proj_biases,
    up_bias,
    cotangent,
):
    count = tokens.shape[1]
    seq_len = segment_ids.shape[1]
    tile = min(512, count)
    me = lax.axis_index("grp")
    rep = lax.axis_index("rep")
    seg_row = segment_ids[0]
    first_row = me * count
    own_seg = lax.dynamic_slice_in_dim(seg_row, first_row, count, 0)
    seg_col = jnp.broadcast_to(own_seg[:, None], (count, 128))
    starts = own_seg[0::tile]
    ends = own_seg[tile - 1 :: tile]
    low = jnp.sum((seg_row[None, :] < starts[:, None]).astype(jnp.int32), axis=1) // count
    high = (jnp.sum((seg_row[None, :] <= ends[:, None]).astype(jnp.int32), axis=1) - 1) // count + 1
    info = jnp.concatenate([me[None].astype(jnp.int32), low, high])
    seg_row = seg_row[None]

    near_qkv = far_rows(w_qkv, rep, size, reps, True, (), (), ())
    first_far, last_far = near_qkv[1][2], near_qkv[-1][2]
    starts_qkv, pieces_qkv = both_cores(near_qkv, swap(w_qkv, "grp", size, 1), size, me, w_qkv.shape[0])
    other_out, other_up, other_down = [swap(weight, "grp", size, 1) for weight in (w_out, w_up, w_down)]
    qkv_full = place_rows(w_qkv, size, starts_qkv, pieces_qkv, key_value_mixed())

    source = tokens[0].astype(F32)
    normed = layer_norm(source, norm_gains[0], norm_shifts[0]).astype(BF16)
    normed_pieces = gather_pieces(after(normed, first_far), size, False, (last_far,), ())
    far_tokens = normed_pieces[1]
    normed_theirs, normed_mine = by_core(normed, me, size)
    normed_all = after(jnp.concatenate(normed_pieces, axis=0), normed_theirs, normed_mine)
    value_bias = proj_biases[1].reshape(PAIRS, LANES)
    bias = jnp.stack([jnp.zeros_like(value_bias), value_bias], axis=1).reshape(-1)
    shift = jnp.concatenate([proj_biases[0], bias])
    qkv_all = (add_rows(normed_all, qkv_full) + shift).astype(BF16)
    heads = (info, qkv_all)
    shapes = (seg_col, seg_row, count, seq_len, size, tile)
    part = PAIRS // 2
    earlier = attend(0, part, *heads, (), (other_out, other_up, other_down), *shapes)
    near_up = far_rows(w_up, rep, size, reps, True, (far_tokens,), earlier, ())
    near_out = far_rows(w_out, rep, size, reps, False, (far_tokens,), earlier, ())
    starts_out, pieces_out = both_cores(near_out, other_out, size, me, w_out.shape[0])
    starts_up, pieces_up = both_cores(near_up, other_up, size, me, w_up.shape[0])
    ready = pieces_out[2:] + pieces_up[2:4]
    attended_f, attended, lse, lse_row = attend(part, part, *heads, earlier, ready, *shapes)
    pieces_out[0], pieces_up[0] = after(pieces_out[0], attended), after(pieces_up[0], attended)
    near_down = far_rows(w_down, rep, size, reps, True, (near_up[1][2],), (attended,), ())
    out_full = place_rows(w_out, size, starts_out, pieces_out)
    middle = source + add_rows(attended, out_full) + proj_biases[2]
    up_full = place_rows(w_up, size, starts_up, pieces_up)
    second = layer_norm(middle, norm_gains[1], norm_shifts[1]).astype(BF16)
    hidden_pre = add_rows(second, up_full) + up_bias
    hidden = jax.nn.gelu(hidden_pre).astype(BF16)
    upstream = cotangent[0]
    upstream_f = upstream.astype(F32)
    hidden_theirs, hidden_mine = by_core(hidden, me, size)
    down_theirs = other_grad(hidden_theirs, upstream)
    near_down = [(near, first, after(piece, hidden)) for near, first, piece in near_down]
    starts_down, pieces_down = both_cores(near_down, other_down, size, me, w_down.shape[0], (down_theirs,))
    down_full = place_rows(w_down, size, starts_down, pieces_down)
    hidden_grad = back_rows(after(upstream, down_theirs), down_full)
    _, gelu_pull = jax.vjp(jax.nn.gelu, hidden_pre)
    pre_grad = gelu_pull(hidden_grad)[0].astype(BF16)
    second_theirs, second_mine = by_core(second, me, size)
    up_theirs = other_grad(second_theirs, pre_grad)
    down_part = core_grad(down_theirs, after(hidden_mine, up_theirs), upstream, size)
    down_send, down_keep = group_step(down_part, bits_of(size) - 1, me)

    up_part = core_grad(up_theirs, second_mine, after(pre_grad, down_send), size)
    up_send, up_keep = rep_halves(up_part, rep)

    second_grad = back_rows(after(pre_grad, up_send), up_full)
    _, second_pull = jax.vjp(layer_norm, middle, norm_gains[1], norm_shifts[1])
    middle_part, gain_second, shift_second = second_pull(second_grad)
    middle_grad = upstream_f + middle_part
    branch_grad = middle_grad.astype(BF16)
    dout = back_rows(branch_grad, out_full).astype(BF16)
    row = lax.broadcasted_iota(jnp.int32, (8 * PAIRS, D), 0)
    minor = row % 8 - 2
    lane_head = lax.broadcasted_iota(jnp.int32, (8 * PAIRS, D), 1) // HD
    picks = ((row // 8 * 2 + minor == lane_head) & (minor >= 0) & (minor < 2)).astype(F32)
    delta_row = jnp.einsum(
        "ed,td->et", picks, dout.astype(F32) * attended_f, precision=lax.Precision.HIGHEST
    ).reshape(PAIRS, 8, count)

    attended_theirs, attended_mine = by_core(after(attended, dout), me, size)
    out_theirs = other_grad(attended_theirs, after(branch_grad, dout))
    queries_one = query_grads(0, part, *heads, after(dout, up_send, out_theirs, delta_row), attended_f, lse, *shapes)

    out_part = core_grad(out_theirs, attended_mine, after(branch_grad, queries_one), size)
    down_part = add_low(down_keep, swap(down_send, "grp", size, size // 2, queries_one))
    down_send, down_keep = rep_halves(group_sum(down_part, me, size)[0], rep)
    up_part = add_low(up_keep, swap(up_send, "rep", reps, 1, queries_one))
    up_send, up_keep = group_step(up_part, bits_of(size) - 1, me)
    queries_two = query_grads(part, part, *heads, after(dout, up_send, down_send, out_part), attended_f, lse, *shapes)
    down_part = add_low(down_keep, swap(down_send, "rep", reps, 1, queries_two))
    up_part = add_low(up_keep, swap(up_send, "grp", size, size // 2, queries_two))
    up_part = group_sum(up_part, me, size)[0]
    both_part = jnp.concatenate([down_part, as_rows(up_part)], axis=0)
    stats = gather_pieces(lse_row + delta_row, size, True, (queries_two,), ())
    dout_all = gather_pieces(dout, size, True, (queries_two,), ())

    both_queries = jnp.concatenate([queries_one, queries_two], axis=1)
    query_theirs = other_grad(normed_theirs, after(both_queries, both_part))
    mixed_one = key_grads(0, part, *heads, [after(dout_all[0], query_theirs, both_part)] + dout_all[1:], stats, *shapes)

    query_part = core_grad(query_theirs, normed_mine, after(both_queries, mixed_one), size)
    pair_part = jnp.concatenate([query_part, out_part], axis=1)
    pair_send, pair_keep = group_step(pair_part, bits_of(size) - 1, me)
    one_theirs = other_grad(normed_theirs, mixed_one)
    both_part = scatter_far(both_part, rep, reps, mixed_one)
    one_part = core_grad(one_theirs, normed_mine, mixed_one, size)
    one_send, one_keep = group_step(one_part, bits_of(size) - 1, me)
    mixed_two = key_grads(
        part, part, *heads, [after(dout_all[0], one_send, pair_send, both_part)] + dout_all[1:], stats, *shapes
    )

    two_theirs = other_grad(normed_theirs, mixed_two)
    two_part = core_grad(two_theirs, normed_mine, mixed_two, size)
    two_send, two_keep = group_step(two_part, bits_of(size) - 1, me)
    one_part = add_low(after(one_keep, two_send), swap(one_send, "grp", size, size // 2, mixed_two))
    pair_part = add_low(after(pair_keep, two_theirs), swap(pair_send, "grp", size, size // 2, mixed_two))
    pair_send, pair_keep = rep_halves(group_sum(pair_part, me, size)[0], rep)
    both_every = share_far(both_part, rep, reps, mixed_two)

    joined_grad = jnp.concatenate([both_queries, mixed_one, mixed_two], axis=1)
    normed_grad = back_rows(after(joined_grad, two_send, pair_send), qkv_full)
    _, first_pull = jax.vjp(layer_norm, source, norm_gains[0], norm_shifts[0])
    source_part, gain_first, shift_first = first_pull(normed_grad)
    input_grad = middle_grad + source_part
    joined_sum = jnp.sum(joined_grad.astype(F32), axis=0, keepdims=True)
    value_sum = joined_sum[:, D:].reshape(PAIRS, 2, LANES)[:, 1].reshape(1, D)
    pre_sum = jnp.sum(pre_grad.astype(F32), axis=0, keepdims=True)
    vectors = jnp.concatenate(
        [
            gain_first[None],
            gain_second[None],
            shift_first[None],
            shift_second[None],
            joined_sum[:, :D],
            value_sum,
            jnp.sum(branch_grad.astype(F32), axis=0, keepdims=True),
            jnp.sum(upstream_f, axis=0, keepdims=True),
            *[pre_sum[:, i : i + D] for i in range(0, FF, D)],
        ],
        axis=0,
    )

    two_part = add_low(two_keep, swap(two_send, "grp", size, size // 2, vectors))
    mixed_part = group_sum(jnp.concatenate([one_part, two_part], axis=1), me, size)[0]
    mixed_send, mixed_keep = rep_halves(mixed_part, rep)
    pair_part = add_low(pair_keep, swap(pair_send, "rep", reps, 1, mixed_send))
    nothing = mixed_send[0:1, :].astype(F32) * 0.0
    block_out = (middle + add_rows(hidden, down_full) + (proj_biases[3] + nothing)).astype(BF16)
    pace = [mixed_send, mixed_send]
    mixed_part = add_low(mixed_keep, swap(mixed_send, "rep", reps, 1, block_out))

    both_got = swap(after(both_every, block_out), "rep", reps, 1)
    pair_part = scatter_far(after(pair_part, mixed_part), rep, reps)
    mixed_part = scatter_far(mixed_part, rep, reps)
    pair_every = share_far(pair_part, rep, reps, mixed_part)
    mixed_every = share_far(mixed_part, rep, reps, pair_every)
    mixed_got = swap(mixed_every, "rep", reps, 1)
    pace += [mixed_part, mixed_every, mixed_got]
    pair_got = swap(pair_every, "rep", reps, 1, mixed_every)
    vectors = total_vector(vectors, size, reps, pace, both_got)

    rows = w_qkv.shape[0]
    tall = w_down.shape[0] // 2
    grad_down = in_order(both_every[:tall], both_got[:tall], rep)
    wide = [
        in_order(both_every[i : i + rows // 2], both_got[i : i + rows // 2], rep)
        for i in range(tall, both_every.shape[0], rows // 2)
    ]
    grad_up = jnp.concatenate(wide, axis=1)
    pair_grad = in_order(pair_every, pair_got, rep).astype(F32)
    mixed_grad = in_order(mixed_every, mixed_got, rep).astype(F32)
    one_keys, one_values = key_value_apart(mixed_grad[:rows])
    two_keys, two_values = key_value_apart(mixed_grad[rows:])
    grad_qkv = jnp.concatenate([pair_grad[:rows]] + one_keys + two_keys + one_values + two_values, axis=1)
    grad_out = pair_grad[rows:]
    return (
        block_out[None],
        input_grad[None],
        grad_qkv,
        grad_out,
        grad_up.astype(F32),
        grad_down.astype(F32),
        vectors[:2],
        vectors[2:4],
        vectors[4:8],
        vectors[8:].reshape(-1),
    )


def solution(mesh):
    return jax.shard_map(
        functools.partial(per_device, mesh.shape["rep"], mesh.shape["grp"]),
        mesh=mesh,
        in_specs=(
            P("rep", "grp", None),
            P("rep", None),
            P("grp", None),
            P("grp", None),
            P("grp", None),
            P("grp", None),
            P(),
            P(),
            P(),
            P(),
            P("rep", "grp", None),
        ),
        out_specs=(
            P("rep", "grp", None),
            P("rep", "grp", None),
            P("grp", None),
            P("grp", None),
            P("grp", None),
            P("grp", None),
            P(),
            P(),
            P(),
            P(),
        ),
        check_vma=False,
    )
```

```python
import functools
import math

import jax
import jax.numpy as jnp
from jax import lax
from jax.experimental import pallas as pl
from jax.experimental.pallas import tpu as pltpu
from jax.sharding import PartitionSpec as P

D = 768
H = 12
HD = 64
FF = 3072
PAIRS = H // 2
LANES = 2 * HD
NEG = -1e30
SCALE = 1.0 / math.sqrt(HD)
F32 = jnp.float32
BF16 = jnp.bfloat16


def layer_norm(values, gain_row, shift_row):
    centre = values - jnp.mean(values, axis=-1, keepdims=True)
    spread = jnp.mean(centre * centre, axis=-1, keepdims=True)
    return centre * lax.rsqrt(spread + 1e-05) * gain_row + shift_row


def add_rows(left, piece):
    return jnp.dot(left, piece, preferred_element_type=F32)


def back_rows(right, piece):
    return jnp.einsum("te,ce->tc", right, piece, preferred_element_type=F32)


def token_product(left, right):
    return jnp.einsum("tc,te->ce", left, right, preferred_element_type=F32)


def after(value, *others):
    return lax.optimization_barrier((value,) + others)[0]


def swap(value, axis, size, mask, *until):
    got = lax.ppermute(value, axis, [(i, i ^ mask) for i in range(size)])
    return after(got, *until) if until else got


def bits_of(size):
    return size.bit_length() - 1


def gather_pieces(value, size, later, until_far, until_core):
    pieces = [value]
    for bit in range(1, bits_of(size)):
        mask = 1 << bit
        pairs = [(i, i ^ mask) for i in range(size) if i & mask or not later]
        pieces += [after(lax.ppermute(piece, "grp", pairs), *until_far) for piece in pieces]
    sent = [after(value, *until_far)] + pieces[1:] if later else pieces
    return pieces + [swap(piece, "grp", size, 1, *until_core) for piece in sent]


def block_place(block, me, size):
    near = block ^ me
    return (near >> 1) | ((near & 1) << (bits_of(size) - 1))


def far_rows(weight, rep, size, reps, spread, before, y_until, x_until):
    rows = weight.shape[0]
    side = rep & 1
    half = rows // 2
    spread = spread and half % 16 == 0
    pieces = [(0, 0, weight)]
    for bit in range(1, bits_of(size)):
        mask = 1 << bit
        found = []
        for near, first, piece in pieces:
            if spread and near == 0:
                part = lax.dynamic_slice_in_dim(piece, side * half, half, 0)
                got = swap(after(part, *before), "grp", size, mask, *y_until)
                found.append((near | mask, side * half, got))
                found.append((near | mask, (1 - side) * half, swap(got, "rep", reps, 1, *x_until)))
            else:
                found.append((near | mask, first, swap(after(piece, *before), "grp", size, mask, *y_until)))
        pieces = pieces + found
    return pieces


def both_cores(pieces, own_other, size, me, rows, until=()):
    starts, found = [], []
    for near, first, piece in pieces:
        starts += [(me ^ near) * rows + first, (me ^ near ^ 1) * rows + first]
        other = own_other if near == 0 else swap(piece, "grp", size, 1, *until)
        found += [piece, other]
    return starts, found


def place_kernel(counts, columns, starts, *refs):
    pieces, (out, sem) = refs[:-2], refs[-2:]
    copies = []
    for i, count in enumerate(counts):
        start = pl.multiple_of(starts[i] * 16, 16)
        for source, target, width in columns:
            copies.append(
                pltpu.make_async_copy(
                    pieces[i].at[:, pl.ds(source, width)],
                    out.at[pl.ds(start, count), pl.ds(target, width)],
                    sem.at[len(copies)],
                )
            )
    for copy in copies:
        copy.start()
    for copy in copies:
        copy.wait()


def place_rows(weight, size, starts, pieces, columns=None):
    rows, width = weight.shape
    counts = [piece.shape[0] for piece in pieces]
    columns = columns or [(0, 0, width)]
    anywhere = pl.BlockSpec(memory_space=pl.ANY)
    return pl.pallas_call(
        functools.partial(place_kernel, counts, columns),
        grid_spec=pltpu.PrefetchScalarGridSpec(
            num_scalar_prefetch=1,
            grid=(1,),
            in_specs=[anywhere] * len(pieces),
            out_specs=pl.BlockSpec((size * rows, width), lambda i, starts: (0, 0)),
            scratch_shapes=[pltpu.SemaphoreType.DMA((len(pieces) * len(columns),))],
        ),
        out_shape=jax.ShapeDtypeStruct((size * rows, width), weight.dtype),
        compiler_params=pltpu.CompilerParams(vmem_limit_bytes=40 * 1024 * 1024),
        cost_estimate=pl.CostEstimate(
            flops=0, bytes_accessed=4 * size * rows * width, transcendentals=0
        ),
    )(jnp.stack(starts).astype(jnp.int32) // 16, *pieces)


def key_value_mixed():
    moves = [(0, 0, D)]
    for pair in range(PAIRS):
        target = D + 2 * LANES * pair
        moves += [(D + LANES * pair, target, LANES), (2 * D + LANES * pair, target + LANES, LANES)]
    return moves


def by_core(left, me, size):
    rows = left.shape[1] // size
    core = me & 1
    if rows % 128 == 0:
        return [
            jnp.concatenate(
                [lax.dynamic_slice_in_dim(left, (2 * i + which) * rows, rows, 1) for i in range(size // 2)], axis=1
            )
            for which in (1 - core, core)
        ]
    strips = [left[:, i * rows : (i + 1) * rows] for i in range(size)]
    even = jnp.concatenate(strips[0::2], axis=1)
    odd = jnp.concatenate(strips[1::2], axis=1)
    return jnp.where(core == 0, odd, even), jnp.where(core == 0, even, odd)


def group_step(part, bit, me):
    size_left, rows, columns = part.shape
    split = part.reshape(2, size_left // 2, rows, columns)
    side = (me >> bit) & 1
    send = lax.dynamic_index_in_dim(split, 1 - side, 0, keepdims=False)
    keep = lax.dynamic_index_in_dim(split, side, 0, keepdims=False)
    return send, keep


def group_sum(part, me, size, *until):
    for bit in range(bits_of(part.shape[0]), 0, -1):
        send, keep = group_step(part, bit, me)
        part = add_low(keep, swap(send, "grp", size, 1 << bit, *until))
    return part


def add_low(keep, got):
    return (keep.astype(F32) + got.astype(F32)).astype(BF16)


def rep_halves(part, rep):
    axis = part.ndim - 2
    half = part.shape[axis] // 2
    side = rep & 1
    send = lax.dynamic_slice_in_dim(part, (1 - side) * half, half, axis)
    keep = lax.dynamic_slice_in_dim(part, side * half, half, axis)
    return send, keep


def scatter_far(part, rep, reps, *until):
    count = reps // 2
    place = rep >> 1
    pieces = part.reshape(count, -1, part.shape[1])
    total = lax.dynamic_index_in_dim(pieces, place, 0, keepdims=False).astype(F32)
    for mask in range(1, count):
        send = lax.dynamic_index_in_dim(pieces, place ^ mask, 0, keepdims=False)
        total = total + swap(send, "rep", reps, mask << 1, *until).astype(F32)
    return total.astype(BF16)


def share_far(own, rep, reps, *until):
    count = reps // 2
    place = rep >> 1
    near = [own] + [swap(own, "rep", reps, mask << 1, *until) for mask in range(1, count)]
    ordered = []
    for i in range(count):
        value = near[i]
        for j in range(1, count):
            value = jnp.where(place == j, near[i ^ j], value)
        ordered.append(value)
    return jnp.concatenate(ordered, axis=0)


def as_rows(part):
    return jnp.concatenate([part[:, i : i + D] for i in range(0, part.shape[1], D)], axis=0)


def in_order(own, got, rep):
    side = rep & 1
    low, high = jnp.where(side == 0, own, got), jnp.where(side == 0, got, own)
    return jnp.concatenate([low, high], axis=0)


def total_vector(value, size, reps, pace, first):
    steps = [("grp", 0), ("rep", 0)] + [("grp", bit) for bit in range(1, bits_of(size))]
    steps += [("rep", bit) for bit in range(1, bits_of(reps))]
    for i, (axis, bit) in enumerate(steps):
        count = size if axis == "grp" else reps
        if (axis, bit) == ("rep", 1):
            value = value + first[0:1, :].astype(F32) * 0.0
        value = value + swap(value, axis, count, 1 << bit, pace[min(i, len(pace) - 1)])
    return value


def other_grad(left, right):
    return token_product(left, right).astype(BF16)


def core_grad(theirs, left, right, size):
    got = swap(theirs, "grp", size, 1).astype(F32)
    part = (token_product(left, right) + got).astype(BF16)
    return part.reshape(size // 2, -1, part.shape[1])


def dot_nt(left, right):
    return lax.dot_general(left, right, (((1,), (1,)), ((), ())), preferred_element_type=F32)


def dot_nn(left, right):
    return lax.dot_general(left, right, (((1,), (0,)), ((), ())), preferred_element_type=F32)


def one_head(pair, head):
    lane = lax.broadcasted_iota(jnp.int32, pair.shape, 1)
    inside = (lane < HD) if head == 0 else (lane >= HD)
    return jnp.where(inside, pair, jnp.zeros_like(pair))


def per_head(first, second, shape):
    lane = lax.broadcasted_iota(jnp.int32, shape, 1)
    return jnp.where(lane < HD, first, second)


def start_of(block, me, size, count):
    return pl.multiple_of(block_place(block, me, size) * count, count)


def query_mask(info, qseg, kseg, bias, tile, count):
    me = info[0]
    for q in range(count // tile):
        rows = pl.ds(q * tile, tile)

        def fill(block, _):
            columns = pl.ds(pl.multiple_of(block * count, count), count)
            q_pos = me * count + q * tile + lax.broadcasted_iota(jnp.int32, (tile, count), 0)
            k_pos = block * count + lax.broadcasted_iota(jnp.int32, (tile, count), 1)
            seen = (k_pos <= q_pos) & (qseg[rows, 0:1] == kseg[0:1, columns])
            bias[rows, columns] = jnp.where(seen, 0.0, NEG)
            return 0

        lax.fori_loop(info[1 + q], me + 1, fill, 0)


def attend_kernel(size, tile, skip, info, q_ref, k_ref, v_ref, qseg, kseg, *refs):
    out, out_low, lse, lse_row, bias = refs[skip:]
    count = q_ref.shape[0]
    me = info[0]

    @pl.when(pl.program_id(0) == 0)
    def _():
        query_mask(info, qseg, kseg, bias, tile, count)

    for q in range(count // tile):
        rows = pl.ds(q * tile, tile)
        queries = q_ref[rows, :] * jnp.asarray(SCALE, BF16)

        def step(block, carry):
            tops, sums, total = carry
            start = start_of(block, me, size, count)
            keys = k_ref[pl.ds(start, count), :]
            values = v_ref[pl.ds(start, count), :]
            add = bias[rows, pl.ds(pl.multiple_of(block * count, count), count)]
            new_tops, new_sums, shrinks = [], [], []
            gain = jnp.zeros((tile, LANES), F32)
            for head in range(2):
                scores = dot_nt(queries, one_head(keys, head)) + add
                top = jnp.maximum(tops[head], jnp.max(scores, axis=1, keepdims=True))
                weights = jnp.exp(scores - top)
                shrink = jnp.exp(tops[head] - top)
                new_tops.append(top)
                shrinks.append(shrink)
                new_sums.append(sums[head] * shrink + jnp.sum(weights, axis=1, keepdims=True))
                gain = gain + dot_nn(weights.astype(BF16), one_head(values, head))
            total = total * per_head(shrinks[0], shrinks[1], total.shape) + gain
            return (tuple(new_tops), tuple(new_sums), total)

        column = jnp.zeros((tile, 1), F32)
        tops, sums, total = lax.fori_loop(
            info[1 + q],
            me + 1,
            step,
            ((column + NEG, column + NEG), (column, column), jnp.zeros((tile, LANES), F32)),
        )
        shape = (tile, LANES)
        result = total / per_head(sums[0], sums[1], shape)
        log_total = per_head(tops[0] + jnp.log(sums[0]), tops[1] + jnp.log(sums[1]), shape)
        out[rows, :] = result
        out_low[rows, :] = result.astype(BF16)
        lse[rows, :] = log_total
        turned = log_total.T
        lse_row[0, :, rows] = jnp.zeros((8, tile), F32)
        lse_row[0, 0:1, rows] = turned[0:1, :]
        lse_row[0, 1:2, rows] = turned[HD : HD + 1, :]


def query_grad_kernel(size, tile, info, q_ref, k_ref, v_ref, dout, out, lse, qseg, kseg, dq, bias):
    count = q_ref.shape[0]
    me = info[0]

    @pl.when(pl.program_id(0) == 0)
    def _():
        query_mask(info, qseg, kseg, bias, tile, count)

    for q in range(count // tile):
        rows = pl.ds(q * tile, tile)
        queries = q_ref[rows, :] * jnp.asarray(SCALE, BF16)
        douts = dout[rows, :]
        both = douts.astype(F32) * out[rows, :]
        deltas = [jnp.sum(one_head(both, head), axis=1, keepdims=True) for head in range(2)]
        logs = [lse[rows, 0:1], lse[rows, HD : HD + 1]]

        def step(block, total):
            start = start_of(block, me, size, count)
            keys = k_ref[pl.ds(start, count), :]
            values = v_ref[pl.ds(start, count), :]
            add = bias[rows, pl.ds(pl.multiple_of(block * count, count), count)]
            for head in range(2):
                one_keys = one_head(keys, head)
                scores = dot_nt(queries, one_keys) + add
                probs = jnp.exp(scores - logs[head])
                prob_grad = dot_nt(douts, one_head(values, head))
                score_grad = (probs * (prob_grad - deltas[head])).astype(BF16)
                total = total + dot_nn(score_grad, one_keys)
            return total

        total = lax.fori_loop(info[1 + q], me + 1, step, jnp.zeros((tile, LANES), F32))
        dq[rows, :] = (total * SCALE).astype(BF16)


def key_grad_kernel(size, tile, info, k_ref, v_ref, q_ref, kseg, qseg, *refs):
    pieces, stat_pieces = refs[:size], refs[size : 2 * size]
    dkv, bias, dout, stats = refs[-4:]
    count = k_ref.shape[0]
    me = info[0]
    for i in range(size):
        dout[pl.ds(i * count, count), :] = pieces[i][...]
        stats[i] = stat_pieces[i][0]
    first = 1 + count // tile

    @pl.when(pl.program_id(0) == 0)
    def _():
        for k in range(count // tile):
            rows = pl.ds(k * tile, tile)

            def fill(block, _):
                columns = pl.ds(pl.multiple_of(block * count, count), count)
                k_pos = me * count + k * tile + lax.broadcasted_iota(jnp.int32, (tile, count), 0)
                q_pos = block * count + lax.broadcasted_iota(jnp.int32, (tile, count), 1)
                seen = (k_pos <= q_pos) & (kseg[rows, 0:1] == qseg[0:1, columns])
                bias[rows, columns] = jnp.where(seen, 0.0, NEG)
                return 0

            lax.fori_loop(me, info[first + k], fill, 0)

    for k in range(count // tile):
        rows = pl.ds(k * tile, tile)
        keys = k_ref[rows, :]
        values = v_ref[rows, :]

        def step(block, carry):
            key_total, value_total = carry
            place = block_place(block, me, size)
            start = pl.multiple_of(place * count, count)
            queries = q_ref[pl.ds(start, count), :] * jnp.asarray(SCALE, BF16)
            douts = dout[pl.ds(start, count), :]
            add = bias[rows, pl.ds(pl.multiple_of(block * count, count), count)]
            for head in range(2):
                one_queries = one_head(queries, head)
                one_douts = one_head(douts, head)
                scores = dot_nt(keys, one_queries) + add
                probs = jnp.exp(scores - stats[place, head : head + 1, :])
                prob_grad = dot_nt(values, one_douts)
                score_grad = probs * (prob_grad - stats[place, 2 + head : 3 + head, :])
                value_total = value_total + dot_nn(probs.astype(BF16), one_douts)
                key_total = key_total + dot_nn(score_grad.astype(BF16), one_queries)
            return (key_total, value_total)

        empty = jnp.zeros((tile, LANES), F32)
        key_total, value_total = lax.fori_loop(me, info[first + k], step, (empty, empty))
        dkv[rows, :LANES] = key_total.astype(BF16)
        dkv[rows, LANES:] = value_total.astype(BF16)


def strip(rows, first, stride=1):
    return pl.BlockSpec((rows, LANES), lambda p, info: (0, first + stride * p))


def whole(shape):
    return pl.BlockSpec(shape, lambda p, info: (0,) * len(shape))


def paired(count, first):
    return pl.BlockSpec((1, 8, count), lambda p, info: (first + p, 0, 0))


def call(body, in_specs, out_specs, out_shape, count, seq_len, products, pairs, mib=60, aliases=None, more_scratch=()):
    return pl.pallas_call(
        body,
        grid_spec=pltpu.PrefetchScalarGridSpec(
            num_scalar_prefetch=1,
            grid=(pairs,),
            in_specs=in_specs,
            out_specs=out_specs,
            scratch_shapes=[pltpu.VMEM((count, seq_len), F32), *more_scratch],
        ),
        out_shape=out_shape,
        input_output_aliases=aliases or {},
        compiler_params=pltpu.CompilerParams(vmem_limit_bytes=mib * 1024 * 1024),
        cost_estimate=pl.CostEstimate(
            flops=products * 2 * count * count * 2 * 256 * 2 * pairs,
            bytes_accessed=8 * 1024 * 1024,
            transcendentals=count * count * 4 * pairs,
        ),
    )


def key_value_strips(rows, first):
    return [strip(rows, PAIRS + 2 * first, 2), strip(rows, PAIRS + 2 * first + 1, 2)]


def attend(first, pairs, info, qkv_all, earlier, ready, seg_col, seg_row, count, seq_len, size, tile):
    out = jax.ShapeDtypeStruct((count, D), F32)
    return call(
        functools.partial(attend_kernel, size, tile, len(earlier) + len(ready)),
        [strip(count, first)]
        + key_value_strips(seq_len, first)
        + [whole((count, 128)), whole((1, seq_len))]
        + [pl.BlockSpec(memory_space=pl.ANY)] * (len(earlier) + len(ready)),
        [strip(count, first), strip(count, first), strip(count, first), paired(count, first)],
        [out, jax.ShapeDtypeStruct((count, D), BF16), out, jax.ShapeDtypeStruct((PAIRS, 8, count), F32)],
        count,
        seq_len,
        2,
        pairs,
        40,
        {6 + i: i for i in range(len(earlier))},
    )(info, qkv_all, qkv_all, qkv_all, seg_col, seg_row, *earlier, *ready)


def query_grads(first, pairs, info, qkv_all, dout, out, lse, seg_col, seg_row, count, seq_len, size, tile):
    return call(
        functools.partial(query_grad_kernel, size, tile),
        [strip(count, first)] + key_value_strips(seq_len, first)
        + [strip(count, first)] * 3
        + [whole((count, 128)), whole((1, seq_len))],
        strip(count, 0),
        jax.ShapeDtypeStruct((count, pairs * LANES), BF16),
        count,
        seq_len,
        3,
        pairs,
    )(info, qkv_all, qkv_all, qkv_all, dout, out, lse, seg_col, seg_row)


def key_grads(first, pairs, info, qkv_all, dout_all, stats, seg_col, seg_row, count, seq_len, size, tile):
    return call(
        functools.partial(key_grad_kernel, size, tile),
        key_value_strips(count, first)
        + [strip(seq_len, first)]
        + [whole((count, 128)), whole((1, seq_len))]
        + [strip(count, first)] * size
        + [paired(count, first)] * size,
        pl.BlockSpec((count, 2 * LANES), lambda p, info: (0, p)),
        jax.ShapeDtypeStruct((count, pairs * 2 * LANES), BF16),
        count,
        seq_len,
        4,
        pairs,
        more_scratch=[pltpu.VMEM((seq_len, LANES), BF16), pltpu.VMEM((size, 8, count), F32)],
    )(info, qkv_all, qkv_all, qkv_all, seg_col, seg_row, *dout_all, *stats)


def key_value_apart(columns):
    rows, width = columns.shape
    strips = [columns[:, i * LANES : (i + 1) * LANES] for i in range(width // LANES)]
    return strips[0::2], strips[1::2]


def per_device(
    reps,
    size,
    tokens,
    segment_ids,
    w_qkv,
    w_out,
    w_up,
    w_down,
    norm_gains,
    norm_shifts,
    proj_biases,
    up_bias,
    cotangent,
):
    count = tokens.shape[1]
    seq_len = segment_ids.shape[1]
    tile = min(512, count)
    me = lax.axis_index("grp")
    rep = lax.axis_index("rep")
    seg_row = segment_ids[0]
    first_row = me * count
    own_seg = lax.dynamic_slice_in_dim(seg_row, first_row, count, 0)
    seg_col = jnp.broadcast_to(own_seg[:, None], (count, 128))
    starts = own_seg[0::tile]
    ends = own_seg[tile - 1 :: tile]
    low = jnp.sum((seg_row[None, :] < starts[:, None]).astype(jnp.int32), axis=1) // count
    high = (jnp.sum((seg_row[None, :] <= ends[:, None]).astype(jnp.int32), axis=1) - 1) // count + 1
    info = jnp.concatenate([me[None].astype(jnp.int32), low, high])
    seg_row = seg_row[None]

    near_qkv = far_rows(w_qkv, rep, size, reps, True, (), (), ())
    first_far, last_far = near_qkv[1][2], near_qkv[-1][2]
    starts_qkv, pieces_qkv = both_cores(near_qkv, swap(w_qkv, "grp", size, 1), size, me, w_qkv.shape[0])
    other_out, other_up, other_down = [swap(weight, "grp", size, 1) for weight in (w_out, w_up, w_down)]
    qkv_full = place_rows(w_qkv, size, starts_qkv, pieces_qkv, key_value_mixed())

    source = tokens[0].astype(F32)
    normed = layer_norm(source, norm_gains[0], norm_shifts[0]).astype(BF16)
    normed_pieces = gather_pieces(after(normed, first_far), size, False, (last_far,), ())
    far_tokens = normed_pieces[1]
    normed_theirs, normed_mine = by_core(normed, me, size)
    normed_all = after(jnp.concatenate(normed_pieces, axis=0), normed_theirs, normed_mine)
    value_bias = proj_biases[1].reshape(PAIRS, LANES)
    bias = jnp.stack([jnp.zeros_like(value_bias), value_bias], axis=1).reshape(-1)
    shift = jnp.concatenate([proj_biases[0], bias])
    qkv_all = (add_rows(normed_all, qkv_full) + shift).astype(BF16)
    heads = (info, qkv_all)
    shapes = (seg_col, seg_row, count, seq_len, size, tile)
    part = PAIRS // 2
    earlier = attend(0, part, *heads, (), (other_out, other_up, other_down), *shapes)
    near_up = far_rows(w_up, rep, size, reps, True, (far_tokens,), earlier, ())
    near_out = far_rows(w_out, rep, size, reps, False, (far_tokens,), earlier, ())
    starts_out, pieces_out = both_cores(near_out, other_out, size, me, w_out.shape[0])
    starts_up, pieces_up = both_cores(near_up, other_up, size, me, w_up.shape[0])
    ready = pieces_out[2:] + pieces_up[2:4]
    attended_f, attended, lse, lse_row = attend(part, part, *heads, earlier, ready, *shapes)
    pieces_out[0], pieces_up[0] = after(pieces_out[0], attended), after(pieces_up[0], attended)
    near_down = far_rows(w_down, rep, size, reps, True, (near_up[1][2],), (attended,), ())
    out_full = place_rows(w_out, size, starts_out, pieces_out)
    middle = source + add_rows(attended, out_full) + proj_biases[2]
    up_full = place_rows(w_up, size, starts_up, pieces_up)
    second = layer_norm(middle, norm_gains[1], norm_shifts[1]).astype(BF16)
    hidden_pre = add_rows(second, up_full) + up_bias
    hidden = jax.nn.gelu(hidden_pre).astype(BF16)
    upstream = cotangent[0]
    upstream_f = upstream.astype(F32)
    hidden_theirs, hidden_mine = by_core(hidden, me, size)
    down_theirs = other_grad(hidden_theirs, upstream)
    near_down = [(near, first, after(piece, hidden)) for near, first, piece in near_down]
    starts_down, pieces_down = both_cores(near_down, other_down, size, me, w_down.shape[0], (down_theirs,))
    down_full = place_rows(w_down, size, starts_down, pieces_down)
    hidden_grad = back_rows(after(upstream, down_theirs), down_full)
    _, gelu_pull = jax.vjp(jax.nn.gelu, hidden_pre)
    pre_grad = gelu_pull(hidden_grad)[0].astype(BF16)
    second_theirs, second_mine = by_core(second, me, size)
    up_theirs = other_grad(second_theirs, pre_grad)
    down_part = core_grad(down_theirs, after(hidden_mine, up_theirs), upstream, size)
    down_send, down_keep = group_step(down_part, bits_of(size) - 1, me)

    up_part = core_grad(up_theirs, second_mine, after(pre_grad, down_send), size)
    up_send, up_keep = rep_halves(up_part, rep)

    second_grad = back_rows(after(pre_grad, up_send), up_full)
    _, second_pull = jax.vjp(layer_norm, middle, norm_gains[1], norm_shifts[1])
    middle_part, gain_second, shift_second = second_pull(second_grad)
    middle_grad = upstream_f + middle_part
    branch_grad = middle_grad.astype(BF16)
    dout = back_rows(branch_grad, out_full).astype(BF16)
    row = lax.broadcasted_iota(jnp.int32, (8 * PAIRS, D), 0)
    minor = row % 8 - 2
    lane_head = lax.broadcasted_iota(jnp.int32, (8 * PAIRS, D), 1) // HD
    picks = ((row // 8 * 2 + minor == lane_head) & (minor >= 0) & (minor < 2)).astype(F32)
    delta_row = jnp.einsum(
        "ed,td->et", picks, dout.astype(F32) * attended_f, precision=lax.Precision.HIGHEST
    ).reshape(PAIRS, 8, count)

    attended_theirs, attended_mine = by_core(after(attended, dout), me, size)
    out_theirs = other_grad(attended_theirs, after(branch_grad, dout))
    queries_one = query_grads(0, part, *heads, after(dout, up_send, out_theirs, delta_row), attended_f, lse, *shapes)

    out_part = core_grad(out_theirs, attended_mine, after(branch_grad, queries_one), size)
    down_part = add_low(down_keep, swap(down_send, "grp", size, size // 2, queries_one))
    down_send, down_keep = rep_halves(group_sum(down_part, me, size)[0], rep)
    up_part = add_low(up_keep, swap(up_send, "rep", reps, 1, queries_one))
    up_send, up_keep = group_step(up_part, bits_of(size) - 1, me)
    queries_two = query_grads(part, part, *heads, after(dout, up_send, down_send, out_part), attended_f, lse, *shapes)
    down_part = add_low(down_keep, swap(down_send, "rep", reps, 1, queries_two))
    up_part = add_low(up_keep, swap(up_send, "grp", size, size // 2, queries_two))
    up_part = group_sum(up_part, me, size)[0]
    both_part = jnp.concatenate([down_part, as_rows(up_part)], axis=0)
    stats = gather_pieces(lse_row + delta_row, size, True, (queries_two,), ())
    dout_all = gather_pieces(dout, size, True, (queries_two,), ())

    both_queries = jnp.concatenate([queries_one, queries_two], axis=1)
    query_theirs = other_grad(normed_theirs, after(both_queries, both_part))
    mixed_one = key_grads(0, part, *heads, [after(dout_all[0], query_theirs, both_part)] + dout_all[1:], stats, *shapes)

    query_part = core_grad(query_theirs, normed_mine, after(both_queries, mixed_one), size)
    one_theirs = other_grad(normed_theirs, mixed_one)
    both_part = scatter_far(both_part, rep, reps, mixed_one)
    one_part = core_grad(one_theirs, normed_mine, mixed_one, size)
    pair_part = jnp.concatenate([query_part, out_part, one_part], axis=1)
    pair_send, pair_keep = group_step(pair_part, bits_of(size) - 1, me)
    mixed_two = key_grads(
        part, part, *heads, [after(dout_all[0], pair_send, both_part)] + dout_all[1:], stats, *shapes
    )

    two_theirs = other_grad(normed_theirs, mixed_two)
    two_part = core_grad(two_theirs, normed_mine, mixed_two, size)
    two_send, two_keep = group_step(two_part, bits_of(size) - 1, me)
    pair_part = add_low(after(pair_keep, two_theirs), swap(pair_send, "grp", size, size // 2, mixed_two))
    pair_rows = 2 * w_qkv.shape[0]
    pair_part, one_part = pair_part[:, :pair_rows], pair_part[:, pair_rows:]
    pair_send, pair_keep = rep_halves(group_sum(pair_part, me, size)[0], rep)
    both_every = share_far(both_part, rep, reps, mixed_two)

    joined_grad = jnp.concatenate([both_queries, mixed_one, mixed_two], axis=1)
    normed_grad = back_rows(after(joined_grad, two_send, pair_send), qkv_full)
    _, first_pull = jax.vjp(layer_norm, source, norm_gains[0], norm_shifts[0])
    source_part, gain_first, shift_first = first_pull(normed_grad)
    input_grad = middle_grad + source_part
    joined_sum = jnp.sum(joined_grad.astype(F32), axis=0, keepdims=True)
    value_sum = joined_sum[:, D:].reshape(PAIRS, 2, LANES)[:, 1].reshape(1, D)
    pre_sum = jnp.sum(pre_grad.astype(F32), axis=0, keepdims=True)
    vectors = jnp.concatenate(
        [
            gain_first[None],
            gain_second[None],
            shift_first[None],
            shift_second[None],
            joined_sum[:, :D],
            value_sum,
            jnp.sum(branch_grad.astype(F32), axis=0, keepdims=True),
            jnp.sum(upstream_f, axis=0, keepdims=True),
            *[pre_sum[:, i : i + D] for i in range(0, FF, D)],
        ],
        axis=0,
    )

    two_part = add_low(two_keep, swap(two_send, "grp", size, size // 2, vectors))
    mixed_part = group_sum(jnp.concatenate([one_part, two_part], axis=1), me, size)[0]
    mixed_send, mixed_keep = rep_halves(mixed_part, rep)
    pair_part = add_low(pair_keep, swap(pair_send, "rep", reps, 1, mixed_send))
    nothing = mixed_send[0:1, :].astype(F32) * 0.0
    block_out = (middle + add_rows(hidden, down_full) + (proj_biases[3] + nothing)).astype(BF16)
    pace = [mixed_send, mixed_send]
    mixed_part = add_low(mixed_keep, swap(mixed_send, "rep", reps, 1, block_out))

    both_got = swap(after(both_every, block_out), "rep", reps, 1)
    pair_part = scatter_far(after(pair_part, mixed_part), rep, reps)
    mixed_part = scatter_far(mixed_part, rep, reps)
    pair_every = share_far(pair_part, rep, reps, mixed_part)
    mixed_every = share_far(mixed_part, rep, reps, pair_every)
    mixed_got = swap(mixed_every, "rep", reps, 1)
    pace += [mixed_part, mixed_every, mixed_got]
    pair_got = swap(pair_every, "rep", reps, 1, mixed_every)
    vectors = total_vector(vectors, size, reps, pace, both_got)

    rows = w_qkv.shape[0]
    tall = w_down.shape[0] // 2
    grad_down = in_order(both_every[:tall], both_got[:tall], rep)
    wide = [
        in_order(both_every[i : i + rows // 2], both_got[i : i + rows // 2], rep)
        for i in range(tall, both_every.shape[0], rows // 2)
    ]
    grad_up = jnp.concatenate(wide, axis=1)
    pair_grad = in_order(pair_every, pair_got, rep).astype(F32)
    mixed_grad = in_order(mixed_every, mixed_got, rep).astype(F32)
    one_keys, one_values = key_value_apart(mixed_grad[:rows])
    two_keys, two_values = key_value_apart(mixed_grad[rows:])
    grad_qkv = jnp.concatenate([pair_grad[:rows]] + one_keys + two_keys + one_values + two_values, axis=1)
    grad_out = pair_grad[rows:]
    return (
        block_out[None],
        input_grad[None],
        grad_qkv,
        grad_out,
        grad_up.astype(F32),
        grad_down.astype(F32),
        vectors[:2],
        vectors[2:4],
        vectors[4:8],
        vectors[8:].reshape(-1),
    )


def solution(mesh):
    return jax.shard_map(
        functools.partial(per_device, mesh.shape["rep"], mesh.shape["grp"]),
        mesh=mesh,
        in_specs=(
            P("rep", "grp", None),
            P("rep", None),
            P("grp", None),
            P("grp", None),
            P("grp", None),
            P("grp", None),
            P(),
            P(),
            P(),
            P(),
            P("rep", "grp", None),
        ),
        out_specs=(
            P("rep", "grp", None),
            P("rep", "grp", None),
            P("grp", None),
            P("grp", None),
            P("grp", None),
            P("grp", None),
            P(),
            P(),
            P(),
            P(),
        ),
        check_vma=False,
    )
```
